512 devices in a mesh: dp: 64 (over y_lo, z, core), mp: 8 (over y_hi, x).
Axes of the slice: x: 4, y: 8 (y_hi: 2, y_lo: 4; y = y_hi * 4 + y_lo), z: 8, core: 2. Of those that a mesh axis runs over, the one named last changes fastest.
Arguments:
- tokens: bfloat16 [3072, 16384], P('dp', 'mp'), may hold values from -6 to 6
- codes: int32 [16384, 8192], P('mp', 'dp'), may hold values from -8 to 7
- expo: int32 [128, 8192], P('mp', 'dp'), may hold values from -4 to -1
- rounding: float32 [16384, 8192], P('mp', 'dp'), may hold values from -6 to 6
- target: bfloat16 [3072, 8192], P(None, 'dp'), may hold values from -32 to 32
Outputs:
- new_rounding: float32 [16384, 8192], P('mp', 'dp')
- loss: float32 [], replicated
The draws below stay inside these ranges and needn't reach their ends.
All inputs are finite; a program needn't handle non-finite values.
Results may differ from the reference program's by a relative error of at most 0.0004.
The reference program's roundings to bfloat16 on the way (of `weights` and `upstream`) count: a program that leaves them out, or rounds other values in their place, can miss the bound.
Values may be sent and summed in bfloat16 or wider, within the bound.
A program may use at most 64 MiB of HBM per device.

```python
import math
import jax
import jax.numpy as jnp
from jax import lax

D = 16384
FW = 8192
GROUP = 128
TOKENS = 3072
N_DP = 64


def draw_target(key, part):
    key = jax.random.fold_in(key, 11)
    key_base, key_col, key_row = jax.random.split(key, 3)
    position = jnp.arange(FW, dtype=jnp.float32) / FW
    base = jnp.clip(jax.random.normal(key_base, (TOKENS, FW), jnp.float32), -6.0, 6.0)
    rise = math.log(3.0)
    row_spread = 0.5 * math.log(10.0)
    amplitude = 0.4
    column = jnp.exp(0.5 * rise * position + jax.random.uniform(key_col, (FW,), jnp.float32, 0.0, 0.5 * math.log(10.0)))
    row_scale = jnp.exp(jax.random.uniform(key_row, (TOKENS, 1), jnp.float32, 0.0, row_spread))
    values = jnp.clip(amplitude * base * column[None, :] * row_scale, -32.0, 32.0)
    return values.astype(jnp.bfloat16)


def touch_ends(drawn, rng, smallest, high):
    shape = drawn.shape
    spot = [jax.random.randint(jax.random.fold_in(rng, axis), (), 0, shape[axis]) for axis in range(len(shape))]
    drawn = drawn.at[tuple(spot)].set(smallest)
    longest = shape.index(max(shape))
    spot[longest] = (spot[longest] + 1) % shape[longest]
    return drawn.at[tuple(spot)].set(high)


def level_of(key, extent, cuts, smallest, high):
    gain = 1.0
    for axis_at, shards_of in cuts:
        draws = jax.random.uniform(jax.random.fold_in(jax.random.fold_in(key, 6), axis_at), (shards_of,), jnp.float32, smallest / len(cuts), high / len(cuts))
        gain = gain * jnp.repeat(jnp.exp(draws), extent[axis_at] // shards_of).reshape((-1,) + (1,) * (len(extent) - 1 - axis_at))
    return gain


def noise(key, dims, scale, reach, cuts=(), held_as=jnp.bfloat16):
    entries = scale * jax.random.normal(key, dims, jnp.float32)
    if cuts:
        entries = entries * level_of(key, dims, cuts, -0.22, 0.18)
    return jnp.clip(entries, -reach, reach).astype(held_as)


def setup_inputs(seed: int = 0) -> dict:
    streams_of = jax.random.split(jax.random.key(seed), 6)
    tokens = noise(streams_of[0], (TOKENS, D), 1.0, 6.0, ((0, 64), (1, 8)))
    codes = touch_ends(jax.random.randint(streams_of[1], (D, FW), -8, 8), jax.random.fold_in(streams_of[1], 1), -8, 7).astype(jnp.int32)
    expo = touch_ends(jax.random.randint(streams_of[2], (D // GROUP, FW), -4, 0), jax.random.fold_in(streams_of[2], 1), -4, -1).astype(jnp.int32)
    rounding = noise(streams_of[3], (D, FW), 1.5, 6.0, ((0, 8), (1, 64)), jnp.float32)
    target = draw_target(jax.random.fold_in(streams_of[5], 71), 0)
    return {"tokens": tokens, "codes": codes, "expo": expo, "rounding": rounding, "target": target}


STRETCH_HIGH = 1.1
STRETCH_LOW = -0.1
LIMIT = 2.3978952727983707
REG_WEIGHT = 0.01
STEP_SIZE = 0.5
EPSILON = 1e-06

def soft_round(rounding):
    sigma = jax.nn.sigmoid(rounding)
    soft = jnp.clip(sigma * (STRETCH_HIGH - STRETCH_LOW) + STRETCH_LOW, 0.0, 1.0)
    slope = jnp.where(jnp.abs(rounding) < LIMIT, (STRETCH_HIGH - STRETCH_LOW) * sigma * (1.0 - sigma), 0.0)
    return (soft, slope)

def group_scale(expo):
    return jnp.repeat(jnp.exp2(expo.astype(jnp.float32)) * D ** (-0.5), GROUP, axis=0)

def reference(tokens, codes, expo, rounding, target):
    target_f = target.astype(jnp.float32)
    energy = jnp.sum(target_f * target_f)
    width = FW // N_DP
    factor = D * FW / energy

    def column_block(index):
        start = index * width
        code_blk = lax.dynamic_slice_in_dim(codes, start, width, 1)
        expo_blk = lax.dynamic_slice_in_dim(expo, start, width, 1)
        round_blk = lax.dynamic_slice_in_dim(rounding, start, width, 1)
        target_blk = lax.dynamic_slice_in_dim(target_f, start, width, 1)
        soft, slope = soft_round(round_blk)
        scale = group_scale(expo_blk)
        weights = (scale * (code_blk.astype(jnp.float32) + soft)).astype(jnp.bfloat16)
        pre = jnp.dot(tokens, weights, preferred_element_type=jnp.float32)
        sigma_pre = jax.nn.sigmoid(pre)
        diff = pre * sigma_pre - target_blk
        upstream = (2.0 * diff * sigma_pre * (1.0 + pre * (1.0 - sigma_pre))).astype(jnp.bfloat16)
        wgrad = lax.dot_general(tokens, upstream, (((0,), (0,)), ((), ())), preferred_element_type=jnp.float32)
        centered = 2.0 * soft - 1.0
        grad = factor * (scale * slope * wgrad) - REG_WEIGHT * 8.0 * centered * centered * centered * slope
        regular = jnp.sum(1.0 - centered * centered * centered * centered)
        return (grad, jnp.sum(diff * diff), regular)
    grads, errors, regulars = lax.map(column_block, jnp.arange(N_DP, dtype=jnp.int32))
    grad_sq = jnp.sum(grads * grads)
    grad_full = jnp.transpose(grads, (1, 0, 2)).reshape(D, FW)
    rms = jnp.sqrt(grad_sq / (D * FW) + EPSILON)
    new_rounding = rounding - STEP_SIZE * grad_full / rms
    loss = jnp.sum(errors) / energy + REG_WEIGHT * jnp.sum(regulars) / (D * FW)
    return (new_rounding, loss)
```

```python
import functools

import jax
import jax.numpy as jnp
from jax import lax
from jax.experimental import pallas as pl
from jax.experimental.pallas import tpu as pltpu
from jax.sharding import PartitionSpec as P

D = 16384
FW = 8192
GROUP = 128
STRETCH_HIGH = 1.1
STRETCH_LOW = -0.1
LIMIT = 2.3978952727983707
REG_WEIGHT = 0.01
STEP_SIZE = 0.5
EPSILON = 1e-06

NX, NYL, NYH, NZ, NC = 4, 4, 2, 8, 2
NQ = NX * NC
NY = NYL * NYH
MESH = pl.DeviceIdType.MESH
F32 = jnp.float32
BF16 = jnp.bfloat16


def rem(a, n):
    return lax.rem(a, jnp.int32(n))


def div(a, n):
    return lax.div(a, jnp.int32(n))


def aligned(a, n):
    return pl.ds(pl.multiple_of(a * n, n), n)


def kernel(
    tokens, codes, expo, rounding, target, out, loss,
    xs, codes_v, expo_v, round_v, tgt, scale_v, ss, reg, grad, w_full, w, part, rbuf, r2, r3, up, gacc, grecv,
    err, red_src, red_buf, energy_v,
    in_sem, tgt_sem, loc_sem, wl_sem, out_sem,
    ys, yr, zs, zr, ws, wr, s1s, s1r, s2s, s2r, s3s, s3r, s4s, s4r, gs, gr, rs, rr,
):
    dp, mp = lax.axis_index("dp"), lax.axis_index("mp")
    core = rem(dp, NC)
    z = rem(div(dp, NC), NZ)
    yl = div(dp, NC * NZ)
    x = rem(mp, NX)
    yh = div(mp, NX)
    q = x * NC + core
    y = yh * NYL + yl

    def dev(x_, yh_, yl_, z_, c_):
        return ((yl_ * NZ + z_) * NC + c_, yh_ * NX + x_)

    rows, kd = tokens.shape
    kh = kd // NC
    blk = rows * NC
    half = blk // NYH
    cols = codes.shape[1]
    groups = kh // GROUP

    def q_dev(o):
        t = rem(q + o, NQ)
        return div(t, NC), rem(t, NC)

    def y_dev(o):
        t = rem(y + o, NY)
        return dev(x, div(t, NYL), rem(t, NYL), z, core)

    def z_dev(o):
        return dev(x, yh, yl, rem(z + o, NZ), core)

    z_up, z_down = z_dev(1), z_dev(NZ - 1)
    sib = dev(x, yh, yl, z, 1 - core)
    y_peer = dev(x, 1 - yh, yl, z, core)

    def copy(src, dst, ssem, rsem, to):
        return pltpu.make_async_remote_copy(
            src_ref=src, dst_ref=dst, send_sem=ssem, recv_sem=rsem, device_id=to, device_id_type=MESH
        )

    loads = [
        pltpu.make_async_copy(rounding, round_v, in_sem.at[0]),
        pltpu.make_async_copy(codes, codes_v, in_sem.at[1]),
        pltpu.make_async_copy(expo, expo_v, in_sem.at[2]),
    ]
    for load in loads:
        load.start()
    for s in range(NZ):
        at = pl.multiple_of(x * (NZ * blk) + s * blk + yh * half, 16)
        pltpu.make_async_copy(target.at[pl.ds(at, half)], tgt.at[s], tgt_sem).start()

    barrier = pltpu.get_barrier_semaphore()
    partners = []
    for o in range(1, NQ):
        x_, c_ = q_dev(o)
        partners.append(dev(x_, yh, yl, z, c_))
    for o in range(1, NY):
        partners.append(y_dev(o))
    for o in range(1, NZ):
        partners.append(z_dev(o))
    for j in range(1, NYL):
        partners.append(dev(x, yh, rem(yl + j, NYL), z, 1 - core))
    for partner in partners:
        pl.semaphore_signal(barrier, inc=1, device_id=partner, device_id_type=MESH)
    pl.semaphore_wait(barrier, len(partners))

    def own_rows(y_, c_):
        return pl.ds(pl.multiple_of(y_ * blk + c_ * rows, 16), rows)

    def token_half(h):
        return tokens.at[:, pl.ds(pl.multiple_of(h * kh, 128), kh)]

    mine = own_rows(yl, core)
    local = pltpu.make_async_copy(token_half(core), xs.at[z, mine], loc_sem)
    local.start()
    copy(token_half(1 - core), xs.at[z, mine], ys, yr.at[yl, core], sib).start()
    for j in range(1, NYL):
        for h in range(NC):
            copy(token_half(h), xs.at[z, mine], ys, yr.at[yl, core], dev(x, yh, rem(yl + j, NYL), z, h)).start()

    def piece(s, y_):
        return xs.at[s, aligned(y_, blk)]

    def forward(s, y_, d, up_flow):
        k, to = (0, z_up) if up_flow else (1, z_down)
        copy(piece(s, y_), piece(s, y_), zs.at[k, d], zr.at[s, y_], to).start()

    def wait_piece(s, y_):
        copy(piece(s, y_), piece(s, y_), zs.at[0, 0], zr.at[s, y_], z_up).wait_recv()

    def down_slab(d):
        return rem(z + NZ - d, NZ)

    def up_slab(d):
        return rem(z + d, NZ)

    def red_send(i, st, value):
        red_src[i, st] = value
        for o in range(1, (NQ, NY, NZ)[st]):
            if st == 0:
                x_, c_ = q_dev(o)
                to = dev(x_, yh, yl, z, c_)
            else:
                to = (y_dev, z_dev)[st - 1](o)
            copy(red_src.at[i, st], red_buf.at[i, st, o - 1], rs.at[i, st], rr.at[i, st], to).start()

    def red_recv(i, st):
        n = (NQ, NY, NZ)[st] - 1
        got = red_buf.at[i, st, pl.ds(0, n)]
        copy(got, got, rs.at[i, st], rr.at[i, st], sib).wait_recv()
        total = red_src[i, st]
        for o in range(n):
            total += red_buf[i, st, o]
        return total

    def red_done(i, st):
        n = (NQ, NY, NZ)[st] - 1
        got = red_buf.at[i, st, pl.ds(0, n)]
        copy(got, got, rs.at[i, st], rr.at[i, st], sib).wait_send()

    def fold(a):
        return a.reshape(a.shape[0] // 8, 8, a.shape[1]).sum(axis=0)

    for load in loads:
        load.wait()
    scale_v[...] = jnp.exp2(expo_v[...].astype(F32)) * D ** (-0.5)

    def group_weights(g, total):
        at = aligned(g, GROUP)
        r = round_v[at]
        sigma = jax.nn.sigmoid(r)
        soft = jnp.clip(sigma * (STRETCH_HIGH - STRETCH_LOW) + STRETCH_LOW, 0.0, 1.0)
        slope = jnp.where(jnp.abs(r) < LIMIT, (STRETCH_HIGH - STRETCH_LOW) * sigma * (1.0 - sigma), 0.0)
        scale = scale_v[pl.ds(g, 1)]
        w_full[at] = (scale * (codes_v[at].astype(F32) + soft)).astype(BF16)
        centered = 2.0 * soft - 1.0
        cube = centered * centered * centered
        ss[at] = scale * slope
        reg[at] = -REG_WEIGHT * 8.0 * cube * slope
        return total + fold(1.0 - cube * centered)

    def half_rows(h):
        return aligned(h, kh)

    def weights(h, total):
        return lax.fori_loop(h * groups, (h + 1) * groups, group_weights, total)

    w_cols = w.at[:, aligned(core, cols)]
    regular = weights(1 - core, jnp.zeros((8, cols), F32))
    send_w = copy(w_full.at[half_rows(1 - core)], w_cols, ws, wr, sib)
    send_w.start()
    regular = weights(core, regular)
    local_w = pltpu.make_async_copy(w_full.at[half_rows(core)], w_cols, wl_sem)
    local_w.start()

    pltpu.make_async_copy(tgt, tgt, tgt_sem).wait()
    err[...] = jnp.zeros_like(err)
    energy = jnp.zeros((8, cols), F32)
    for s in range(NZ):
        t = tgt[s].astype(F32)
        energy += fold(t * t)
    red_send(0, 0, energy)
    gacc[...] = jnp.zeros_like(gacc)

    def s1(s):
        def rows_of(j, carry):
            at = aligned(j, blk)
            part[s, at] = jnp.dot(xs[s, at], w[...], preferred_element_type=F32)
            return carry

        lax.fori_loop(0, NYL, rows_of, 0)
        for o in range(1, NQ):
            x_, c_ = q_dev(o)
            copy(
                part.at[s, aligned(x_, blk), aligned(c_, cols)], rbuf.at[s, o - 1], s1s.at[s], s1r.at[s],
                dev(x_, yh, yl, z, c_),
            ).start()

    def s2(s):
        copy(rbuf.at[s], rbuf.at[s], s1s.at[s], s1r.at[s], sib).wait_recv()
        total = part[s, aligned(x, blk), aligned(core, cols)]
        for o in range(NQ - 1):
            total += rbuf[s, o]
        for i in range(NYH):
            r2[s, i] = total[i * half : (i + 1) * half]
        copy(r2.at[s, 1 - yh], r3.at[s], s2s.at[s], s2r.at[s], y_peer).start()

    def up_at(s):
        return up.at[s, pl.ds(pl.multiple_of(x * blk + yh * half, 16), half), aligned(core, cols)]

    def s3(s):
        copy(r3.at[s], r3.at[s], s2s.at[s], s2r.at[s], y_peer).wait_recv()
        pre = r2[s, yh] + r3[s]
        sigma = jax.nn.sigmoid(pre)
        diff = pre * sigma - tgt[s].astype(F32)
        up_at(s)[...] = (2.0 * diff * sigma * (1.0 + pre * (1.0 - sigma))).astype(BF16)
        err[...] += fold(diff * diff)
        copy(up_at(s), up_at(s), s3s.at[s], s3r.at[s], y_peer).start()

    def s4(s):
        copy(up_at(s), up_at(s), s3s.at[s], s3r.at[s], y_peer).wait_recv()
        src = up.at[s, aligned(x, blk), aligned(core, cols)]
        for o in range(1, NQ):
            x_, c_ = q_dev(o)
            copy(src, src, s4s.at[s], s4r.at[s], dev(x_, yh, yl, z, c_)).start()

    def seven(s):
        return up.at[s, pl.ds(0, (NQ - 1) * blk // NC)]

    def s5(s):
        copy(seven(s), seven(s), s4s.at[s], s4r.at[s], sib).wait_recv()
        u = up[s].T

        def cols_of(i, carry):
            at = aligned(i, 256 if kh % 256 == 0 else 128)
            gacc[:, at] += jnp.dot(u, xs[s, :, at], preferred_element_type=F32)
            return carry

        lax.fori_loop(0, kh // (256 if kh % 256 == 0 else 128), cols_of, 0)

    for j in range(NYL):
        y_ = rem(yl + j, NYL)
        if j == 0:
            local.wait()
            at = own_rows(yl, 1 - core)
            copy(xs.at[z, at], xs.at[z, at], ys, yr.at[yl, 1 - core], sib).wait_recv()
        else:
            for c_ in range(NC):
                at = own_rows(y_, c_)
                copy(xs.at[z, at], xs.at[z, at], ys, yr.at[y_, c_], sib).wait_recv()
        forward(z, y_, 0, True)
        forward(z, y_, 0, False)
    red_send(0, 1, red_recv(0, 0))
    local_w.wait()
    send_w.wait_recv()
    s1(z)
    red_send(0, 2, red_recv(0, 1))
    total = red_recv(0, 2)
    energy_v[...] = jnp.broadcast_to(jnp.sum(total, axis=(0, 1), keepdims=True), energy_v.shape)

    last = NZ // 2

    def each(d, fn):
        def go(i, carry):
            fn(rem(z + NZ + (2 * i - 1) * d, NZ))
            return carry

        lax.fori_loop(0, jnp.where(d == 0, 1, 2), go, 0)

    stages = (s2, s3, s4, s5)

    def step(d, carry):
        below, above = down_slab(d), up_slab(d)
        for j in range(NYL):
            y_ = rem(yl + j, NYL)
            wait_piece(below, y_)
            if j < NYL // 2:
                forward(below, y_, d, True)
            else:
                pl.when(d < last - 1)(functools.partial(forward, below, y_, d, True))
            wait_piece(above, y_)
            if j >= NYL // 2:
                forward(above, y_, d, False)
            else:
                pl.when(d < last - 1)(functools.partial(forward, above, y_, d, False))
            if j < len(stages):
                each(d - 1, stages[j])
        for stage in stages[NYL:]:
            each(d - 1, stage)
        each(d, s1)
        return carry

    lax.fori_loop(1, last, step, 0)

    far = up_slab(last)
    prev = last - 1
    for j in range(NYL // 2):
        wait_piece(far, rem(yl + j, NYL))
        wait_piece(far, rem(yl + j + NYL // 2, NYL))
        each(prev, stages[j])
    s1(far)
    for stage in stages[NYL // 2 :]:
        each(prev, stage)
    for stage in stages:
        stage(far)

    send_g = copy(gacc.at[aligned(1 - core, cols)], grecv, gs, gr, sib)
    send_g.start()
    factor = float(D * FW) / energy_v[0:1, 0:1]

    def finish(ref, first, h):
        def go(i, total):
            at = aligned(h * groups + i, GROUP)
            wgrad = ref[pl.ds(first, cols), aligned(i, GROUP)].T
            g = factor * (ss[at] * wgrad) + reg[at]
            grad[at] = g
            return total + fold(g * g)

        return functools.partial(lax.fori_loop, 0, groups, go)

    squares = finish(gacc, pl.multiple_of(core * cols, cols), core)(jnp.zeros((8, cols), F32))
    send_g.wait_recv()
    squares = finish(grecv, 0, 1 - core)(squares)

    row = lax.broadcasted_iota(jnp.int32, (8, cols), 0)
    parts = [jnp.sum(v, axis=0, keepdims=True) for v in (squares, err[...], regular)]
    tile = jnp.zeros((8, cols), F32)
    for i, v in enumerate(parts):
        tile = jnp.where(row == i, v, tile)
    red_send(1, 0, tile)
    red_send(1, 1, red_recv(1, 0))
    red_send(1, 2, red_recv(1, 1))
    sums = jnp.sum(red_recv(1, 2), axis=1, keepdims=True)
    rms = jnp.sqrt(sums[0:1] / float(D * FW) + EPSILON)
    inverse = STEP_SIZE / rms
    loss[...] = sums[1:2] / energy_v[0:1, 0:1] + REG_WEIGHT * sums[2:3] / float(D * FW)

    def result(g, carry):
        at = aligned(g, GROUP)
        round_v[at] = round_v[at] - grad[at] * inverse
        return carry

    lax.fori_loop(0, NC * groups, result, 0)
    store = pltpu.make_async_copy(round_v, out, out_sem)
    store.start()

    all_rows = xs.at[0, pl.ds(0, (2 * NYL - 1) * rows)]
    copy(all_rows, all_rows, ys, yr.at[0, 0], sib).wait_send()
    for k in range(2):
        for d in range(last):
            n = NYL * blk if d < last - 1 else NYL * blk // 2
            sent = xs.at[0, pl.ds(0, n)]
            copy(sent, sent, zs.at[k, d], zr.at[0, 0], z_up).wait_send()
    send_w.wait_send()
    send_g.wait_send()

    def sent_stages(s, carry):
        copy(rbuf.at[s], rbuf.at[s], s1s.at[s], s1r.at[s], sib).wait_send()
        copy(r3.at[s], r3.at[s], s2s.at[s], s2r.at[s], y_peer).wait_send()
        copy(up_at(s), up_at(s), s3s.at[s], s3r.at[s], y_peer).wait_send()
        copy(seven(s), seven(s), s4s.at[s], s4r.at[s], sib).wait_send()
        return carry

    lax.fori_loop(0, NZ, sent_stages, 0)
    for i in range(2):
        for st in range(3):
            red_done(i, st)
    store.wait()


def local(tokens, codes, expo, rounding, target):
    rows, kd = tokens.shape
    cols = codes.shape[1]
    kh = kd // NC
    blk = rows * NC
    half = blk // NYH
    slab = NYL * blk
    dma = pltpu.SemaphoreType.DMA
    vmem = pltpu.VMEM
    out, loss = pl.pallas_call(
        kernel,
        out_shape=(
            jax.ShapeDtypeStruct(rounding.shape, F32),
            jax.ShapeDtypeStruct((1, 1), F32),
        ),
        in_specs=[pl.BlockSpec(memory_space=pl.ANY)] * 5,
        out_specs=(pl.BlockSpec(memory_space=pl.ANY), pl.BlockSpec(memory_space=pltpu.VMEM)),
        scratch_shapes=[
            vmem((NZ, slab, kh), BF16),
            vmem((kd, cols), jnp.int32),
            vmem(expo.shape, jnp.int32),
            vmem((kd, cols), F32),
            vmem((NZ, half, cols), BF16),
            vmem(expo.shape, F32),
            vmem((kd, cols), F32),
            vmem((kd, cols), F32),
            vmem((kd, cols), F32),
            vmem((kd, cols), BF16),
            vmem((kh, NC * cols), BF16),
            vmem((NZ, slab, NC * cols), F32),
            vmem((NZ, NQ - 1, blk, cols), F32),
            vmem((NZ, NYH, half, cols), F32),
            vmem((NZ, half, cols), F32),
            vmem((NZ, slab, NC * cols), BF16),
            vmem((NC * cols, kh), F32),
            vmem((cols, kh), F32),
            vmem((8, cols), F32),
            vmem((2, 3, 8, cols), F32),
            vmem((2, 3, max(NQ, NY, NZ) - 1, 8, cols), F32),
            vmem((8, cols), F32),
            dma((3,)), dma, dma, dma, dma,
            dma, dma((NYL, NC)), dma((2, NZ // 2)), dma((NZ, NYL)), dma, dma,
            dma((NZ,)), dma((NZ,)), dma((NZ,)), dma((NZ,)), dma((NZ,)), dma((NZ,)), dma((NZ,)), dma((NZ,)),
            dma, dma, dma((2, 3)), dma((2, 3)),
        ],
        compiler_params=pltpu.CompilerParams(
            collective_id=0, has_side_effects=True, vmem_limit_bytes=48 * 1024 * 1024
        ),
    )(tokens, codes, expo, rounding, target)
    return out, loss.reshape(())


def solution(mesh):
    in_specs = (P("dp", "mp"), P("mp", "dp"), P("mp", "dp"), P("mp", "dp"), P(None, "dp"))
    out_specs = (P("mp", "dp"), P())
    return jax.shard_map(local, mesh=mesh, in_specs=in_specs, out_specs=out_specs, check_vma=False)
```

```python
import functools

import jax
import jax.numpy as jnp
from jax import lax
from jax.experimental import pallas as pl
from jax.experimental.pallas import tpu as pltpu
from jax.sharding import PartitionSpec as P

D = 16384
FW = 8192
GROUP = 128
STRETCH_HIGH = 1.1
STRETCH_LOW = -0.1
LIMIT = 2.3978952727983707
REG_WEIGHT = 0.01
STEP_SIZE = 0.5
EPSILON = 1e-06

NX, NYL, NYH, NZ, NC = 4, 4, 2, 8, 2
NQ = NX * NC
NY = NYL * NYH
B_COLS = 128

PLAN = (((1, 2),), (), ((2, 4), (1, 3)), ((3, 5), (0, 1)))
FAR = (((1, 2), (2, 4)), ())
TAIL = ((0, 1), (1, 3), (0, 2), (3, 5), (2, 5), (0, 3), (1, 4), (0, 4), (1, 5), (0, 5))
MESH = pl.DeviceIdType.MESH
F32 = jnp.float32
BF16 = jnp.bfloat16


def rem(a, n):
    return lax.rem(a, jnp.int32(n))


def div(a, n):
    return lax.div(a, jnp.int32(n))


def aligned(a, n):
    return pl.ds(pl.multiple_of(a * n, n), n)


def kernel(
    tokens, codes, expo, rounding, target, out, loss,
    xs, codes_v, expo_v, round_v, tgt, scale_v, ss, reg, grad, w_full, w, part, sbuf, rbuf, r2, r3, up, gacc, grecv,
    err, red_src, red_buf, energy_v,
    in_sem, tgt_sem, loc_sem, wl_sem, out_sem,
    ts, tr, bs, br, zf, za, zb, zr, ws, wr, s1s, s1r, s2s, s2r, s3s, s3r, s4s, s4r, gs, gr, rs, rr,
):
    dp, mp = lax.axis_index("dp"), lax.axis_index("mp")
    core = rem(dp, NC)
    z = rem(div(dp, NC), NZ)
    yl = div(dp, NC * NZ)
    x = rem(mp, NX)
    yh = div(mp, NX)
    q = x * NC + core
    y = yh * NYL + yl

    def dev(x_, yh_, yl_, z_, c_):
        return ((yl_ * NZ + z_) * NC + c_, yh_ * NX + x_)

    rows, kd = tokens.shape
    kh = kd // NC
    blk = rows * NC
    cols = codes.shape[1]
    groups = kh // GROUP
    a_cols = kh - B_COLS
    last = NZ // 2

    def q_dev(o):
        t = rem(q + o, NQ)
        return dev(div(t, NC), yh, yl, z, rem(t, NC))

    def y_dev(o):
        t = rem(y + o, NY)
        return dev(x, div(t, NYL), rem(t, NYL), z, core)

    def z_dev(o):
        return dev(x, yh, yl, rem(z + o, NZ), core)

    def x_dev(o):
        return dev(rem(x + o, NX), yh, yl, z, core)

    z_next = (z_dev(1), z_dev(NZ - 1))
    line_next = (dev(x, yh, rem(yl + 1, NYL), z, core), dev(x, yh, rem(yl + NYL - 1, NYL), z, core))
    has_next = (yl < NYL - 1, yl > 0)
    sib = dev(x, yh, yl, z, 1 - core)
    y_peer = dev(x, 1 - yh, yl, z, core)

    def copy(src, dst, ssem, rsem, to):
        return pltpu.make_async_remote_copy(
            src_ref=src, dst_ref=dst, send_sem=ssem, recv_sem=rsem, device_id=to, device_id_type=MESH
        )

    def same(ref, ssem, rsem, to):
        return copy(ref, ref, ssem, rsem, to)

    loads = [
        pltpu.make_async_copy(rounding, round_v, in_sem.at[0]),
        pltpu.make_async_copy(codes, codes_v, in_sem.at[1]),
        pltpu.make_async_copy(expo, expo_v, in_sem.at[2]),
    ]
    for load in loads:
        load.start()
    for s in range(NZ):
        at = pl.multiple_of(x * (NZ * blk) + s * blk, 16)
        pltpu.make_async_copy(target.at[pl.ds(at, blk)], tgt.at[s], tgt_sem).start()

    def token_half(h):
        return tokens.at[:, aligned(h, kh)]

    def own_rows(c_):
        return pl.ds(pl.multiple_of(yl * blk + c_ * rows, 16), rows)

    local = pltpu.make_async_copy(token_half(core), xs.at[z, own_rows(core)], loc_sem)
    local.start()

    barrier = pltpu.get_barrier_semaphore()
    partners = [q_dev(o) for o in range(1, NQ)] + [y_dev(o) for o in range(1, NY)] + [z_dev(o) for o in range(1, NZ)]
    for partner in partners:
        pl.semaphore_signal(barrier, inc=1, device_id=partner, device_id_type=MESH)
    pl.semaphore_wait(barrier, len(partners))

    send_t = copy(token_half(1 - core), xs.at[z, own_rows(core)], ts, tr, sib)
    send_t.start()

    def piece(s, y_):
        return xs.at[s, aligned(y_, blk)]

    def a_piece(s, y_):
        return xs.at[s, aligned(y_, blk), pl.ds(0, a_cols)]

    def b_piece(s, y_):
        return xs.at[s, aligned(y_, blk), pl.ds(a_cols, B_COLS)]

    def z_send(s, j, y_, d, k):
        if j == 0:
            same(piece(s, y_), zf.at[k, d], zr.at[s, y_], z_next[k]).start()
        else:
            same(a_piece(s, y_), za.at[k, d], zr.at[s, y_], z_next[k]).start()

    def z_wait(s, j, y_):
        same((a_piece if j else piece)(s, y_), zf.at[0, 0], zr.at[s, y_], sib).wait_recv()

    def line_send(s, y_, side, ref):
        @pl.when(has_next[side])
        def _():
            same(ref(s, y_), bs.at[side, s, y_], br.at[s, y_], line_next[side]).start()

    def line_pass(s, j, ref, then):
        for side in range(2):
            y_ = yl - j if side == 0 else yl + j

            @pl.when(y_ >= 0 if side == 0 else y_ < NYL)
            def _(side=side, y_=y_):
                same(ref(s, y_), bs.at[side, s, y_], br.at[s, y_], sib).wait_recv()
                line_send(s, y_, side, ref)
                then(y_)

    def red_send(i, st, value):
        red_src[i, st] = value
        for o in range(1, (NQ, NY, NZ)[st]):
            to = (q_dev, y_dev, z_dev)[st](o)
            copy(red_src.at[i, st], red_buf.at[i, st, o - 1], rs.at[i, st], rr.at[i, st], to).start()

    def red_got(i, st):
        n = (NQ, NY, NZ)[st] - 1
        return same(red_buf.at[i, st, pl.ds(0, n)], rs.at[i, st], rr.at[i, st], sib)

    def red_recv(i, st):
        red_got(i, st).wait_recv()
        total = red_src[i, st]
        for o in range((NQ, NY, NZ)[st] - 1):
            total += red_buf[i, st, o]
        return total

    def fold(a):
        return a.reshape(a.shape[0] // 8, 8, a.shape[1]).sum(axis=0)

    local.wait()
    send_t_back = copy(token_half(1 - core), xs.at[z, own_rows(1 - core)], ts, tr, sib)
    send_t_back.wait_recv()
    for k in range(2):
        z_send(z, 0, yl, 0, k)
        line_send(z, yl, k, piece)

    for load in loads:
        load.wait()
    scale_v[...] = jnp.exp2(expo_v[...].astype(F32)) * D ** (-0.5)

    def group_weights(g, total):
        at = aligned(g, GROUP)
        r = round_v[at]
        sigma = jax.nn.sigmoid(r)
        soft = jnp.clip(sigma * (STRETCH_HIGH - STRETCH_LOW) + STRETCH_LOW, 0.0, 1.0)
        slope = jnp.where(jnp.abs(r) < LIMIT, (STRETCH_HIGH - STRETCH_LOW) * sigma * (1.0 - sigma), 0.0)
        scale = scale_v[pl.ds(g, 1)]
        w_full[at] = (scale * (codes_v[at].astype(F32) + soft)).astype(BF16)
        centered = 2.0 * soft - 1.0
        cube = centered * centered * centered
        ss[at] = scale * slope
        reg[at] = -REG_WEIGHT * 8.0 * cube * slope
        return total + fold(1.0 - cube * centered)

    def half_rows(h):
        return aligned(h, kh)

    def weights(h, total):
        return lax.fori_loop(h * groups, (h + 1) * groups, group_weights, total)

    w_cols = w.at[:, aligned(core, cols)]
    regular = weights(1 - core, jnp.zeros((8, cols), F32))
    send_w = copy(w_full.at[half_rows(1 - core)], w_cols, ws, wr, sib)
    send_w.start()
    regular = weights(core, regular)
    local_w = pltpu.make_async_copy(w_full.at[half_rows(core)], w_cols, wl_sem)
    local_w.start()

    pltpu.make_async_copy(tgt, tgt, tgt_sem).wait()
    err[...] = jnp.zeros_like(err)
    energy = jnp.zeros((8, cols), F32)
    for s in range(NZ):
        t = tgt[s].astype(F32)
        energy += fold(t * t)
    red_send(0, 0, energy)
    gacc[...] = jnp.zeros_like(gacc)

    own_cols, sib_cols = aligned(core, cols), aligned(1 - core, cols)
    own_x = aligned(x, blk)

    def t1(s):
        def rows_of(j, carry):
            at = aligned(j, blk)
            part[s, at] = jnp.dot(xs[s, at], w[...], preferred_element_type=F32)
            return carry

        lax.fori_loop(0, NYL, rows_of, 0)
        copy(part.at[s, :, sib_cols], sbuf.at[s], s1s.at[s], s1r.at[s], sib).start()

    def t2(s):
        same(sbuf.at[s], s1s.at[s], s1r.at[s], sib).wait_recv()
        sbuf[s] = sbuf[s] + part[s, :, own_cols]
        for o in range(1, NX):
            src = sbuf.at[s, aligned(rem(x + o, NX), blk)]
            copy(src, rbuf.at[s, o - 1], s2s.at[s], s2r.at[s], x_dev(o)).start()

    def t3(s):
        same(rbuf.at[s], s2s.at[s], s2r.at[s], sib).wait_recv()
        total = sbuf[s, own_x]
        for o in range(NX - 1):
            total += rbuf[s, o]
        r2[s] = total
        copy(r2.at[s], r3.at[s], s3s.at[s], s3r.at[s], y_peer).start()

    def t4(s):
        same(r3.at[s], s3s.at[s], s3r.at[s], y_peer).wait_recv()
        pre = r2[s] + r3[s]
        sigma = jax.nn.sigmoid(pre)
        diff = pre * sigma - tgt[s].astype(F32)
        up[s, own_x, own_cols] = (2.0 * diff * sigma * (1.0 + pre * (1.0 - sigma))).astype(BF16)
        err[...] += fold(diff * diff)
        for o in range(1, NQ):
            same(up.at[s, own_x, own_cols], s4s.at[s], s4r.at[s], q_dev(o)).start()

    def seven(s):
        return same(up.at[s, pl.ds(0, (NQ - 1) * blk // NC)], s4s.at[s], s4r.at[s], sib)

    wide = min(kh, 256)

    def t5(s):
        seven(s).wait_recv()
        u = up[s].T

        def cols_of(i, carry):
            at = aligned(i, wide)
            gacc[:, at] += jnp.dot(u, xs[s, :, at], preferred_element_type=F32)
            return carry

        lax.fori_loop(0, kh // wide, cols_of, 0)

    def each(d, stage):
        def go(i, carry):
            (t1, t2, t3, t4, t5)[stage - 1](rem(z + NZ + (2 * i - 1) * d, NZ))
            return carry

        lax.fori_loop(0, jnp.where(d > 0, 2, jnp.where(d == 0, 1, 0)), go, 0)

    def at_far(back, stage):
        if back:
            each(jnp.int32(last - back), stage)
        else:
            (t1, t2, t3, t4, t5)[stage - 1](far)

    def energy_stage(st):
        if st < 3:
            red_send(0, st, red_recv(0, st - 1))
        else:
            total = red_recv(0, 2)
            energy_v[...] = jnp.broadcast_to(jnp.sum(total, axis=(0, 1), keepdims=True) * (1.0 / NYH), energy_v.shape)

    def none(y_):
        return None

    def tick(d, j):
        slabs = rem(z + NZ - d, NZ), rem(z + d, NZ)

        def take(rel, y_):
            for k in range(2):
                z_wait(slabs[k], rel, y_)
                if (rel < NYL // 2) == (k == 0):
                    z_send(slabs[k], rel, y_, d, k)
                else:
                    pl.when(d < last - 1)(functools.partial(z_send, slabs[k], rel, y_, d, k))

        if j == 0:
            take(0, yl)
            for s in slabs:
                for side in range(2):
                    line_send(s, yl, side, b_piece)
        else:
            pl.when(yl >= j)(functools.partial(take, NYL - j, yl - j))
            pl.when(yl + j < NYL)(functools.partial(take, j, yl + j))
            for s in slabs:
                line_pass(s, j, b_piece, none)
        if j == NYL - 1:

            @pl.when(d == last - 1)
            def _():
                for i in range(1, NYL):
                    k = 0 if i < NYL // 2 else 1
                    at = rem(yl + i, NYL)
                    same(b_piece(slabs[k], at), zb.at[k], br.at[slabs[k], at], z_next[k]).start()

    for j in range(1, NYL):

        def onward(y_):
            for k in range(2):
                z_send(z, 1, y_, 0, k)

        line_pass(z, j, piece, onward)
        tick(jnp.int32(1), j - 1)
    local_w.wait()
    send_w.wait_recv()
    t1(z)
    tick(jnp.int32(1), NYL - 1)
    energy_stage(1)
    t2(z)
    each(jnp.int32(1), 1)

    def step(d, carry):
        for j in range(NYL):
            tick(d, j)
            if j == 0:
                pl.when(d == 2)(functools.partial(t3, z))
            for back, stage in PLAN[j]:
                each(d - back, stage)
            if j == NYL - 1:
                for st in range(2, 4):
                    if st < last:
                        pl.when(d == st)(functools.partial(energy_stage, st))
        return carry

    lax.fori_loop(2, last, step, 0)

    far = rem(z + last, NZ)
    for j in range(NYL // 2):
        for jj in (j, j + NYL // 2):
            z_wait(far, jj, rem(yl + jj, NYL))
        for work in FAR[j]:
            at_far(*work)
    for j in range(1, NYL):
        at = rem(yl + j, NYL)
        same(b_piece(far, at), zb.at[0], br.at[far, at], sib).wait_recv()
    if last == 2:
        t3(z)
    for st in range(last, 4):
        energy_stage(st)
    for work in TAIL:
        at_far(*work)

    send_g = copy(gacc.at[sib_cols], grecv, gs, gr, sib)
    send_g.start()
    factor = float(D * FW) / energy_v[0:1, 0:1]

    def finish(ref, first, h):
        def go(i, total):
            at = aligned(h * groups + i, GROUP)
            wgrad = ref[pl.ds(first, cols), aligned(i, GROUP)].T
            g = factor * (ss[at] * wgrad) + reg[at]
            grad[at] = g
            return total + fold(g * g)

        return functools.partial(lax.fori_loop, 0, groups, go)

    squares = finish(gacc, pl.multiple_of(core * cols, cols), core)(jnp.zeros((8, cols), F32))
    send_g.wait_recv()
    squares = finish(grecv, 0, 1 - core)(squares)

    row = lax.broadcasted_iota(jnp.int32, (8, cols), 0)
    parts = [jnp.sum(v, axis=0, keepdims=True) for v in (squares, err[...] * (1.0 / NYH), regular)]
    tile = jnp.zeros((8, cols), F32)
    for i, v in enumerate(parts):
        tile = jnp.where(row == i, v, tile)
    red_send(1, 0, tile)
    red_send(1, 1, red_recv(1, 0))
    red_send(1, 2, red_recv(1, 1))
    sums = jnp.sum(red_recv(1, 2), axis=1, keepdims=True)
    rms = jnp.sqrt(sums[0:1] / float(D * FW) + EPSILON)
    inverse = STEP_SIZE / rms
    loss[...] = sums[1:2] / energy_v[0:1, 0:1] + REG_WEIGHT * sums[2:3] / float(D * FW)

    def result(g, carry):
        at = aligned(g, GROUP)
        round_v[at] = round_v[at] - grad[at] * inverse
        return carry

    lax.fori_loop(0, NC * groups, result, 0)
    store = pltpu.make_async_copy(round_v, out, out_sem)
    store.start()

    send_t.wait_send()
    for k in range(2):
        for d in range(last):
            n = NYL - 1
            if d < last - 1 or k == 0:
                same(piece(z, yl), zf.at[k, d], zr.at[z, yl], sib).wait_send()
            if d == last - 1:
                n = NYL // 2 - 1 if k == 0 else NYL - NYL // 2
                if n:
                    same(xs.at[z, pl.ds(0, n * blk), pl.ds(0, B_COLS)], zb.at[k], zr.at[z, yl], sib).wait_send()
            if n:
                same(xs.at[z, pl.ds(0, n * blk), pl.ds(0, a_cols)], za.at[k, d], zr.at[z, yl], sib).wait_send()

    def sent_line(s, ref):
        for side in range(2):
            for y_ in range(NYL):

                @pl.when(jnp.logical_and(has_next[side], y_ <= yl if side == 0 else y_ >= yl))
                def _(side=side, y_=y_):
                    same(ref(s, y_), bs.at[side, s, y_], br.at[s, y_], sib).wait_send()

    sent_line(z, piece)

    def sent_far_line(d, carry):
        for s in (rem(z + NZ - d, NZ), rem(z + d, NZ)):
            sent_line(s, b_piece)
        return carry

    lax.fori_loop(1, last, sent_far_line, 0)
    send_w.wait_send()
    send_g.wait_send()

    def sent_stages(s, carry):
        same(sbuf.at[s], s1s.at[s], s1r.at[s], sib).wait_send()
        same(rbuf.at[s], s2s.at[s], s2r.at[s], sib).wait_send()
        same(r3.at[s], s3s.at[s], s3r.at[s], y_peer).wait_send()
        seven(s).wait_send()
        return carry

    lax.fori_loop(0, NZ, sent_stages, 0)
    for i in range(2):
        for st in range(3):
            red_got(i, st).wait_send()
    store.wait()


def local(tokens, codes, expo, rounding, target):
    rows, kd = tokens.shape
    cols = codes.shape[1]
    kh = kd // NC
    blk = rows * NC
    slab = NYL * blk
    dma = pltpu.SemaphoreType.DMA
    vmem = pltpu.VMEM
    out, loss = pl.pallas_call(
        kernel,
        out_shape=(
            jax.ShapeDtypeStruct(rounding.shape, F32),
            jax.ShapeDtypeStruct((1, 1), F32),
        ),
        in_specs=[pl.BlockSpec(memory_space=pl.ANY)] * 5,
        out_specs=(pl.BlockSpec(memory_space=pl.ANY), pl.BlockSpec(memory_space=pltpu.VMEM)),
        scratch_shapes=[
            vmem((NZ, slab, kh), BF16),
            vmem((kd, cols), jnp.int32),
            vmem(expo.shape, jnp.int32),
            vmem((kd, cols), F32),
            vmem((NZ, blk, cols), BF16),
            vmem(expo.shape, F32),
            vmem((kd, cols), F32),
            vmem((kd, cols), F32),
            vmem((kd, cols), F32),
            vmem((kd, cols), BF16),
            vmem((kh, NC * cols), BF16),
            vmem((NZ, slab, NC * cols), F32),
            vmem((NZ, slab, cols), F32),
            vmem((NZ, NX - 1, blk, cols), F32),
            vmem((NZ, blk, cols), F32),
            vmem((NZ, blk, cols), F32),
            vmem((NZ, slab, NC * cols), BF16),
            vmem((NC * cols, kh), F32),
            vmem((cols, kh), F32),
            vmem((8, cols), F32),
            vmem((2, 3, 8, cols), F32),
            vmem((2, 3, max(NQ, NY, NZ) - 1, 8, cols), F32),
            vmem((8, cols), F32),
            dma((3,)), dma, dma, dma, dma,
            dma, dma, dma((2, NZ, NYL)), dma((NZ, NYL)), dma((2, NZ // 2)), dma((2, NZ // 2)), dma((2,)), dma((NZ, NYL)), dma, dma,
            dma((NZ,)), dma((NZ,)), dma((NZ,)), dma((NZ,)), dma((NZ,)), dma((NZ,)), dma((NZ,)), dma((NZ,)),
            dma, dma, dma((2, 3)), dma((2, 3)),
        ],
        compiler_params=pltpu.CompilerParams(
            collective_id=0, has_side_effects=True, vmem_limit_bytes=60 * 1024 * 1024
        ),
    )(tokens, codes, expo, rounding, target)
    return out, loss.reshape(())


def solution(mesh):
    in_specs = (P("dp", "mp"), P("mp", "dp"), P("mp", "dp"), P("mp", "dp"), P(None, "dp"))
    out_specs = (P("mp", "dp"), P())
    return jax.shard_map(local, mesh=mesh, in_specs=in_specs, out_specs=out_specs, check_vma=False)
```

```python
import functools

import jax
import jax.numpy as jnp
from jax import lax
from jax.experimental import pallas as pl
from jax.experimental.pallas import tpu as pltpu
from jax.sharding import PartitionSpec as P

D = 16384
FW = 8192
GROUP = 128
STRETCH_HIGH = 1.1
STRETCH_LOW = -0.1
LIMIT = 2.3978952727983707
REG_WEIGHT = 0.01
STEP_SIZE = 0.5
EPSILON = 1e-06

NX, NYL, NYH, NZ, NC = 4, 4, 2, 8, 2
NQ = NX * NC
NY = NYL * NYH
B_COLS = 128

PLAN = (((1, 2),), ((3, 5),), ((1, 3),), ((2, 4), (0, 1)))
BEFORE_FAR = ((1, 2),)
FAR = (((2, 4), (3, 5)), ())
TAIL = ((0, 1), (1, 3), (0, 2), (2, 5), (0, 3), (1, 4), (0, 4), (1, 5), (0, 5))
MESH = pl.DeviceIdType.MESH


def by_distance(n):
    return sorted(range(1, n), key=lambda o: -min(o, n - o))


VMEM_LIMIT = 60 << 20
F32 = jnp.float32
BF16 = jnp.bfloat16


def rem(a, n):
    return lax.rem(a, jnp.int32(n))


def div(a, n):
    return lax.div(a, jnp.int32(n))


def aligned(a, n):
    return pl.ds(pl.multiple_of(a * n, n), n)


def kernel(
    tokens, codes, expo, rounding, target, grad, inverse, loss,
    xs, codes_v, expo_v, round_v, tgt, scale_v, ss, reg, ss_sib, reg_sib, grad_sib, w_full, w, part, sbuf, rbuf, r2, r3, up, gacc,
    err, red_src, red_buf, energy_v,
    in_sem, tgt_sem, loc_sem, wl_sem,
    ts, tr, tz, tl, bs, bb, br, zf, za, zb, zr, ws, wr, fs, fr, s1s, s1r, s2s, s2r, s3s, s3r, s4s, s4r, gs, gr, rs, rr,
):
    dp, mp = lax.axis_index("dp"), lax.axis_index("mp")
    core = rem(dp, NC)
    z = rem(div(dp, NC), NZ)
    yl = div(dp, NC * NZ)
    x = rem(mp, NX)
    yh = div(mp, NX)
    q = x * NC + core
    y = yh * NYL + yl

    def dev(x_, yh_, yl_, z_, c_):
        return ((yl_ * NZ + z_) * NC + c_, yh_ * NX + x_)

    rows, kd = tokens.shape
    kh = kd // NC
    blk = rows * NC
    cols = codes.shape[1]
    groups = kh // GROUP
    a_cols = kh - B_COLS
    last = NZ // 2

    def q_dev(o):
        t = rem(q + o, NQ)
        return dev(div(t, NC), yh, yl, z, rem(t, NC))

    def y_dev(o):
        t = rem(y + o, NY)
        return dev(x, div(t, NYL), rem(t, NYL), z, core)

    def z_dev(o):
        return dev(x, yh, yl, rem(z + o, NZ), core)

    def x_dev(o):
        return dev(rem(x + o, NX), yh, yl, z, core)

    z_next = (z_dev(1), z_dev(NZ - 1))
    line_next = (dev(x, yh, rem(yl + 1, NYL), z, core), dev(x, yh, rem(yl + NYL - 1, NYL), z, core))
    has_next = (yl < NYL - 1, yl > 0)
    sib = dev(x, yh, yl, z, 1 - core)
    y_peer = dev(x, 1 - yh, yl, z, core)

    def copy(src, dst, ssem, rsem, to):
        return pltpu.make_async_remote_copy(
            src_ref=src, dst_ref=dst, send_sem=ssem, recv_sem=rsem, device_id=to, device_id_type=MESH
        )

    def core_of(to, c_):
        return (to[0] - core + c_, to[1])

    def same(ref, ssem, rsem, to):
        return copy(ref, ref, ssem, rsem, to)

    loads = [
        pltpu.make_async_copy(rounding, round_v, in_sem.at[0]),
        pltpu.make_async_copy(codes, codes_v, in_sem.at[1]),
        pltpu.make_async_copy(expo, expo_v, in_sem.at[2]),
    ]
    for load in loads:
        load.start()
    for s in range(NZ):
        at = pl.multiple_of(x * (NZ * blk) + s * blk, 16)
        pltpu.make_async_copy(target.at[pl.ds(at, blk)], tgt.at[s], tgt_sem).start()

    def token_half(h):
        return tokens.at[:, aligned(h, kh)]

    def own_rows(c_):
        return pl.ds(pl.multiple_of(yl * blk + c_ * rows, 16), rows)

    local = pltpu.make_async_copy(token_half(core), xs.at[z, own_rows(core)], loc_sem)
    local.start()

    barrier = pltpu.get_barrier_semaphore()
    partners = [q_dev(o) for o in range(1, NQ)] + [y_dev(o) for o in range(1, NY)] + [z_dev(o) for o in range(1, NZ)]
    partners += [core_of(to, 1 - core) for to in z_next + line_next]
    for partner in partners:
        pl.semaphore_signal(barrier, inc=1, device_id=partner, device_id_type=MESH)
    pl.semaphore_wait(barrier, len(partners))

    mine = xs.at[z, own_rows(core)]
    for k, to in enumerate(z_next):
        for h in range(NC):
            copy(token_half(h), mine, zf.at[k, 0], tz.at[k, core], core_of(to, h)).start()
    for side, to in enumerate(line_next):

        @pl.when(has_next[side])
        def _(side=side, to=to):
            for h in range(NC):
                copy(token_half(h), mine, bs.at[side, yl], tl.at[side, core], core_of(to, h)).start()

    send_t = copy(token_half(1 - core), mine, ts, tr, sib)
    send_t.start()

    def both_cores(s, y_, sems):
        for c_ in range(NC):
            at = pl.ds(pl.multiple_of(y_ * blk + c_ * rows, 16), rows)
            same(xs.at[s, at], ts, sems.at[c_], sib).wait_recv()

    def piece(s, y_):
        return xs.at[s, aligned(y_, blk)]

    def a_piece(s, y_):
        return xs.at[s, aligned(y_, blk), pl.ds(0, a_cols)]

    def b_piece(s, y_):
        return xs.at[s, aligned(y_, blk), pl.ds(a_cols, B_COLS)]

    def place(p):
        found = yl
        for at in range(NYL):
            order = sorted(range(NYL), key=lambda y_: (abs(y_ - at), y_))
            found = jnp.where(yl == at, order[p], found)
        return found

    def z_send(s, j, y_, d, k):
        if j == 0:
            same(piece(s, y_), zf.at[k, d], zr.at[s, y_], z_next[k]).start()
        else:
            same(a_piece(s, y_), za.at[k, d], zr.at[s, y_], z_next[k]).start()

    def z_wait(s, j, y_):
        same((a_piece if j else piece)(s, y_), zf.at[0, 0], zr.at[s, y_], sib).wait_recv()

    def line_send(y_, side):
        @pl.when(has_next[side])
        def _():
            same(piece(z, y_), bs.at[side, y_], br.at[z, y_], line_next[side]).start()

    def line_pass(j, then):
        for side in range(2):
            y_ = yl - j if side == 0 else yl + j

            @pl.when(y_ >= 0 if side == 0 else y_ < NYL)
            def _(side=side, y_=y_):
                if j == 1:
                    both_cores(z, y_, tl.at[side])
                else:
                    same(piece(z, y_), bs.at[side, y_], br.at[z, y_], sib).wait_recv()
                line_send(y_, side)
                then(y_)

    def red_send(i, st, value):
        red_src[i, st] = value
        for o in by_distance((NQ, NY, NZ)[st]):
            to = (q_dev, y_dev, z_dev)[st](o)
            copy(red_src.at[i, st], red_buf.at[i, st, o - 1], rs.at[i, st], rr.at[i, st], to).start()

    def red_got(i, st):
        n = (NQ, NY, NZ)[st] - 1
        return same(red_buf.at[i, st, pl.ds(0, n)], rs.at[i, st], rr.at[i, st], sib)

    def red_recv(i, st):
        red_got(i, st).wait_recv()
        total = red_src[i, st]
        for o in range((NQ, NY, NZ)[st] - 1):
            total += red_buf[i, st, o]
        return total

    def fold(a):
        return a.reshape(a.shape[0] // 8, 8, a.shape[1]).sum(axis=0)

    for load in loads:
        load.wait()
    scale_v[...] = jnp.exp2(expo_v[...].astype(F32)) * D ** (-0.5)

    def group_weights(g, total):
        at = aligned(g, GROUP)
        r = round_v[at]
        sigma = jax.nn.sigmoid(r)
        soft = jnp.clip(sigma * (STRETCH_HIGH - STRETCH_LOW) + STRETCH_LOW, 0.0, 1.0)
        slope = jnp.where(jnp.abs(r) < LIMIT, (STRETCH_HIGH - STRETCH_LOW) * sigma * (1.0 - sigma), 0.0)
        scale = scale_v[pl.ds(g, 1)]
        w_full[at] = (scale * (codes_v[at].astype(F32) + soft)).astype(BF16)
        centered = 2.0 * soft - 1.0
        cube = centered * centered * centered
        ss[at] = scale * slope
        reg[at] = -REG_WEIGHT * 8.0 * cube * slope
        return total + fold(1.0 - cube * centered)

    def half_rows(h):
        return aligned(h, kh)

    def weights(h, total):
        return lax.fori_loop(h * groups, (h + 1) * groups, group_weights, total)

    w_cols = w.at[:, aligned(core, cols)]
    regular = weights(1 - core, jnp.zeros((8, cols), F32))
    send_w = copy(w_full.at[half_rows(1 - core)], w_cols, ws, wr, sib)
    send_w.start()
    send_slopes = [
        copy(ref.at[half_rows(1 - core)], other, fs.at[i], fr.at[i], sib)
        for i, (ref, other) in enumerate(((ss, ss_sib), (reg, reg_sib)))
    ]
    for send in send_slopes:
        send.start()
    regular = weights(core, regular)
    local_w = pltpu.make_async_copy(w_full.at[half_rows(core)], w_cols, wl_sem)
    local_w.start()

    pltpu.make_async_copy(tgt, tgt, tgt_sem).wait()
    err[...] = jnp.zeros_like(err)
    energy = jnp.zeros((8, cols), F32)
    for s in range(NZ):
        t = tgt[s].astype(F32)
        energy += fold(t * t)
    red_send(0, 0, energy)
    gacc[...] = jnp.zeros_like(gacc)

    own_cols, sib_cols = aligned(core, cols), aligned(1 - core, cols)
    own_x = aligned(x, blk)

    def t1(s):
        def rows_of(j, carry):
            at = aligned(j, blk)
            part[s, at] = jnp.dot(xs[s, at], w[...], preferred_element_type=F32)
            return carry

        lax.fori_loop(0, NYL, rows_of, 0)
        copy(part.at[s, :, sib_cols], sbuf.at[s], s1s.at[s], s1r.at[s], sib).start()

    def t2(s):
        same(sbuf.at[s], s1s.at[s], s1r.at[s], sib).wait_recv()
        sbuf[s] = sbuf[s] + part[s, :, own_cols]
        for o in by_distance(NX):
            src = sbuf.at[s, aligned(rem(x + o, NX), blk)]
            copy(src, rbuf.at[s, o - 1], s2s.at[s], s2r.at[s], x_dev(o)).start()

    def t3(s):
        same(rbuf.at[s], s2s.at[s], s2r.at[s], sib).wait_recv()
        total = sbuf[s, own_x]
        for o in range(NX - 1):
            total += rbuf[s, o]
        r2[s] = total
        copy(r2.at[s], r3.at[s], s3s.at[s], s3r.at[s], y_peer).start()

    def t4(s):
        same(r3.at[s], s3s.at[s], s3r.at[s], y_peer).wait_recv()
        pre = r2[s] + r3[s]
        sigma = jax.nn.sigmoid(pre)
        diff = pre * sigma - tgt[s].astype(F32)
        up[s, own_x, own_cols] = (2.0 * diff * sigma * (1.0 + pre * (1.0 - sigma))).astype(BF16)
        err[...] += fold(diff * diff)
        for o in by_distance(NQ):
            same(up.at[s, own_x, own_cols], s4s.at[s], s4r.at[s], q_dev(o)).start()

    def seven(s):
        return same(up.at[s, pl.ds(0, (NQ - 1) * blk // NC)], s4s.at[s], s4r.at[s], sib)

    wide = min(kh, 256)

    def t5(s):
        seven(s).wait_recv()
        u = up[s].T

        def cols_of(i, carry):
            at = aligned(i, wide)
            gacc[:, at] += jnp.dot(u, xs[s, :, at], preferred_element_type=F32)
            return carry

        lax.fori_loop(0, kh // wide, cols_of, 0)

    def each(d, stage):
        def go(i, carry):
            (t1, t2, t3, t4, t5)[stage - 1](rem(z + NZ + (2 * i - 1) * d, NZ))
            return carry

        lax.fori_loop(0, jnp.where(d > 0, 2, jnp.where(d == 0, 1, 0)), go, 0)

    def at_far(back, stage):
        if back:
            each(jnp.int32(last - back), stage)
        else:
            (t1, t2, t3, t4, t5)[stage - 1](far)

    def energy_stage(st):
        if st < 3:
            red_send(0, st, red_recv(0, st - 1))
        else:
            total = red_recv(0, 2)
            energy_v[...] = jnp.broadcast_to(jnp.sum(total, axis=(0, 1), keepdims=True) * (1.0 / NYH), energy_v.shape)

    def tick(d, j, first=False):
        slabs = rem(z + NZ - d, NZ), rem(z + d, NZ)
        y_ = place(j)
        for k in range(2):
            if first:
                both_cores(slabs[k], y_, tz.at[k])
            else:
                z_wait(slabs[k], j, y_)
            if (j < NYL // 2) == (k == 0):
                z_send(slabs[k], j, y_, d, k)
            else:
                pl.when(d < last - 1)(functools.partial(z_send, slabs[k], j, y_, d, k))
        if j == 0:
            for s in slabs:
                for o in range(1, NYL):
                    to = dev(x, yh, rem(yl + o, NYL), z, core)
                    same(b_piece(s, yl), bb.at[s, o], br.at[s, yl], to).start()
        if j == NYL - 1:
            for s in slabs:
                for o in range(1, NYL):
                    at = rem(yl + o, NYL)
                    same(b_piece(s, at), bb.at[s, o], br.at[s, at], sib).wait_recv()

            @pl.when(d == last - 1)
            def _():
                for i in range(1, NYL):
                    k = 0 if i < NYL // 2 else 1
                    at = place(i)
                    same(b_piece(slabs[k], at), zb.at[k], br.at[slabs[k], at], z_next[k]).start()

    for j in range(1, NYL):

        def onward(y_):
            for k in range(2):
                z_send(z, 1, y_, 0, k)

        line_pass(j, onward)
        tick(jnp.int32(1), j - 1, j == 1)
    local_w.wait()
    send_w.wait_recv()
    local.wait()
    copy(token_half(1 - core), xs.at[z, own_rows(1 - core)], ts, tr, sib).wait_recv()
    t1(z)
    tick(jnp.int32(1), NYL - 1)
    energy_stage(1)
    t2(z)
    for back, stage in PLAN[NYL - 1]:
        if back == 0:
            each(jnp.int32(1), stage)

    def step(d, carry):
        for j in range(NYL):
            tick(d, j)
            if j == 0:
                pl.when(d == 2)(functools.partial(t3, z))
            for back, stage in PLAN[j]:
                each(d - back, stage)
            if j == NYL - 1:
                for st in range(2, 4):
                    if st < last:
                        pl.when(d == st)(functools.partial(energy_stage, st))
        return carry

    lax.fori_loop(2, last, step, 0)

    far = rem(z + last, NZ)
    for work in BEFORE_FAR:
        at_far(*work)
    for j in range(NYL // 2):
        for jj in (j, j + NYL // 2):
            z_wait(far, jj, place(jj))
        for work in FAR[j]:
            at_far(*work)
    for j in range(1, NYL):
        at = rem(yl + j, NYL)
        same(b_piece(far, at), zb.at[0], br.at[far, at], sib).wait_recv()
    if last == 2:
        t3(z)
    for st in range(last, 4):
        energy_stage(st)
    for work in TAIL:
        at_far(*work)

    factor = float(D * FW) / energy_v[0:1, 0:1]
    for send in send_slopes:
        send.wait_recv()

    def finish(first, slopes, reg_ref, into, base):
        def go(i, total):
            at = aligned(base + i, GROUP)
            g = factor * (slopes[at] * gacc[pl.ds(first, cols), aligned(i, GROUP)].T) + reg_ref[at]
            into[at] = g
            return total + fold(g * g)

        return functools.partial(lax.fori_loop, 0, groups, go)

    sib_first, own_first = (pl.multiple_of(c_ * cols, cols) for c_ in (1 - core, core))
    squares = finish(sib_first, ss_sib, reg_sib, grad_sib, 0)(jnp.zeros((8, cols), F32))
    send_g = copy(grad_sib, grad.at[half_rows(core)], gs, gr, sib)
    send_g.start()
    squares = finish(own_first, ss, reg, grad, core * groups)(squares)

    row = lax.broadcasted_iota(jnp.int32, (8, cols), 0)
    parts = [jnp.sum(v, axis=0, keepdims=True) for v in (squares, err[...] * (1.0 / NYH), regular)]
    tile = jnp.zeros((8, cols), F32)
    for i, v in enumerate(parts):
        tile = jnp.where(row == i, v, tile)
    red_send(1, 0, tile)
    send_g.wait_recv()
    red_send(1, 1, red_recv(1, 0))
    red_send(1, 2, red_recv(1, 1))
    sums = jnp.sum(red_recv(1, 2), axis=1, keepdims=True)
    rms = jnp.sqrt(sums[0:1] / float(D * FW) + EPSILON)
    inverse[...] = STEP_SIZE / rms
    loss[...] = sums[1:2] / energy_v[0:1, 0:1] + REG_WEIGHT * sums[2:3] / float(D * FW)

    send_t.wait_send()
    for k in range(2):
        for d in range(last):
            n = NYL - 1
            if d < last - 1 or k == 0:
                same(piece(z, yl), zf.at[k, d], zr.at[z, yl], sib).wait_send()
            if d == last - 1:
                n = NYL // 2 - 1 if k == 0 else NYL - NYL // 2
                if n:
                    same(xs.at[z, pl.ds(0, n * blk), pl.ds(0, B_COLS)], zb.at[k], zr.at[z, yl], sib).wait_send()
            if n:
                same(xs.at[z, pl.ds(0, n * blk), pl.ds(0, a_cols)], za.at[k, d], zr.at[z, yl], sib).wait_send()

    for side in range(2):
        for y_ in range(NYL):

            @pl.when(jnp.logical_and(has_next[side], y_ <= yl if side == 0 else y_ >= yl))
            def _(side=side, y_=y_):
                same(piece(z, y_), bs.at[side, y_], br.at[z, y_], sib).wait_send()

    def sent_far_line(d, carry):
        for s in (rem(z + NZ - d, NZ), rem(z + d, NZ)):
            for o in range(1, NYL):
                same(b_piece(s, yl), bb.at[s, o], br.at[s, yl], sib).wait_send()
        return carry

    lax.fori_loop(1, last, sent_far_line, 0)
    send_w.wait_send()
    send_g.wait_send()
    for send in send_slopes:
        send.wait_send()

    def sent_stages(s, carry):
        same(sbuf.at[s], s1s.at[s], s1r.at[s], sib).wait_send()
        same(rbuf.at[s], s2s.at[s], s2r.at[s], sib).wait_send()
        same(r3.at[s], s3s.at[s], s3r.at[s], y_peer).wait_send()
        seven(s).wait_send()
        return carry

    lax.fori_loop(0, NZ, sent_stages, 0)
    for i in range(2):
        for st in range(3):
            red_got(i, st).wait_send()


def local(tokens, codes, expo, rounding, target):
    rows, kd = tokens.shape
    cols = codes.shape[1]
    kh = kd // NC
    blk = rows * NC
    slab = NYL * blk
    dma = pltpu.SemaphoreType.DMA
    vmem = pltpu.VMEM
    grad, inverse, loss = pl.pallas_call(
        kernel,
        out_shape=(
            jax.ShapeDtypeStruct(rounding.shape, F32),
            jax.ShapeDtypeStruct((1, 1), F32),
            jax.ShapeDtypeStruct((1, 1), F32),
        ),
        in_specs=[pl.BlockSpec(memory_space=pl.ANY)] * 5,
        out_specs=(pl.BlockSpec(memory_space=pltpu.VMEM),) * 3,
        scratch_shapes=[
            vmem((NZ, slab, kh), BF16),
            vmem((kd, cols), jnp.int32),
            vmem(expo.shape, jnp.int32),
            vmem((kd, cols), F32),
            vmem((NZ, blk, cols), BF16),
            vmem(expo.shape, F32),
            vmem((kd, cols), F32),
            vmem((kd, cols), F32),
            vmem((kh, cols), F32),
            vmem((kh, cols), F32),
            vmem((kh, cols), F32),
            vmem((kd, cols), BF16),
            vmem((kh, NC * cols), BF16),
            vmem((NZ, slab, NC * cols), F32),
            vmem((NZ, slab, cols), F32),
            vmem((NZ, NX - 1, blk, cols), F32),
            vmem((NZ, blk, cols), F32),
            vmem((NZ, blk, cols), F32),
            vmem((NZ, slab, NC * cols), BF16),
            vmem((NC * cols, kh), F32),
            vmem((8, cols), F32),
            vmem((2, 3, 8, cols), F32),
            vmem((2, 3, max(NQ, NY, NZ) - 1, 8, cols), F32),
            vmem((8, cols), F32),
            dma((3,)), dma, dma, dma,
            dma, dma, dma((2, NC)), dma((2, NC)), dma((2, NYL)), dma((NZ, NYL)), dma((NZ, NYL)), dma((2, NZ // 2)), dma((2, NZ // 2)), dma((2,)), dma((NZ, NYL)), dma, dma,
            dma((2,)), dma((2,)), dma((NZ,)), dma((NZ,)), dma((NZ,)), dma((NZ,)), dma((NZ,)), dma((NZ,)), dma((NZ,)), dma((NZ,)),
            dma, dma, dma((2, 3)), dma((2, 3)),
        ],
        compiler_params=pltpu.CompilerParams(
            collective_id=0, has_side_effects=True, vmem_limit_bytes=VMEM_LIMIT
        ),
    )(tokens, codes, expo, rounding, target)
    return rounding - grad * inverse, loss.reshape(())


def solution(mesh):
    in_specs = (P("dp", "mp"), P("mp", "dp"), P("mp", "dp"), P("mp", "dp"), P(None, "dp"))
    out_specs = (P("mp", "dp"), P())
    return jax.shard_map(local, mesh=mesh, in_specs=in_specs, out_specs=out_specs, check_vma=False)
```

```python
import functools

import jax
import jax.numpy as jnp
from jax import lax
from jax.experimental import pallas as pl
from jax.experimental.pallas import tpu as pltpu
from jax.sharding import PartitionSpec as P

D = 16384
FW = 8192
GROUP = 128
STRETCH_HIGH = 1.1
STRETCH_LOW = -0.1
LIMIT = 2.3978952727983707
REG_WEIGHT = 0.01
STEP_SIZE = 0.5
EPSILON = 1e-06

NX, NYL, NYH, NZ, NC = 4, 4, 2, 8, 2
NQ = NX * NC
NY = NYL * NYH
B_COLS = 128

PLAN = (((1, 2),), ((3, 5),), ((1, 3),), ((2, 4), (0, 1)))
BEFORE_FAR = ((1, 2),)
FAR = (((2, 4), (3, 5)), ())
TAIL = ((0, 1), (1, 3), (0, 2), (2, 5), (0, 3), (1, 4), (0, 4), (1, 5), (0, 5))
MESH = pl.DeviceIdType.MESH


def by_distance(n):
    return sorted(range(1, n), key=lambda o: -min(o, n - o))


VMEM_LIMIT = 60 << 20
F32 = jnp.float32
BF16 = jnp.bfloat16


def rem(a, n):
    return lax.rem(a, jnp.int32(n))


def div(a, n):
    return lax.div(a, jnp.int32(n))


def aligned(a, n):
    return pl.ds(pl.multiple_of(a * n, n), n)


def kernel(
    tokens, codes, expo, rounding, target, grad, inverse, loss,
    xs, codes_v, expo_v, round_v, tgt, scale_v, ss, reg, ss_sib, reg_sib, grad_sib, w_full, w, part, sbuf, rbuf, r2, r3, up, gacc,
    err, red_src, red_buf, energy_v,
    in_sem, tgt_sem, loc_sem, wl_sem,
    ts, tr, tz, tl, bs, bb, br, zf, za, zb, zr, ws, wr, fs, fr, s1s, s1r, s2s, s2r, s3s, s3r, s4s, s4r, gs, gr, rs, rr,
):
    dp, mp = lax.axis_index("dp"), lax.axis_index("mp")
    core = rem(dp, NC)
    z = rem(div(dp, NC), NZ)
    yl = div(dp, NC * NZ)
    x = rem(mp, NX)
    yh = div(mp, NX)
    q = x * NC + core
    y = yh * NYL + yl

    def dev(x_, yh_, yl_, z_, c_):
        return ((yl_ * NZ + z_) * NC + c_, yh_ * NX + x_)

    rows, kd = tokens.shape
    kh = kd // NC
    blk = rows * NC
    cols = codes.shape[1]
    groups = kh // GROUP
    a_cols = kh - B_COLS
    last = NZ // 2

    def q_dev(o):
        t = rem(q + o, NQ)
        return dev(div(t, NC), yh, yl, z, rem(t, NC))

    def y_dev(o):
        t = rem(y + o, NY)
        return dev(x, div(t, NYL), rem(t, NYL), z, core)

    def z_dev(o):
        return dev(x, yh, yl, rem(z + o, NZ), core)

    def x_dev(o):
        return dev(rem(x + o, NX), yh, yl, z, core)

    z_next = (z_dev(1), z_dev(NZ - 1))
    line_next = (dev(x, yh, rem(yl + 1, NYL), z, core), dev(x, yh, rem(yl + NYL - 1, NYL), z, core))
    has_next = (yl < NYL - 1, yl > 0)
    sib = dev(x, yh, yl, z, 1 - core)
    y_peer = dev(x, 1 - yh, yl, z, core)

    def copy(src, dst, ssem, rsem, to):
        return pltpu.make_async_remote_copy(
            src_ref=src, dst_ref=dst, send_sem=ssem, recv_sem=rsem, device_id=to, device_id_type=MESH
        )

    def core_of(to, c_):
        return (to[0] - core + c_, to[1])

    def same(ref, ssem, rsem, to):
        return copy(ref, ref, ssem, rsem, to)

    barrier = pltpu.get_barrier_semaphore()
    partners = [y_dev(o) for o in by_distance(NY)] + [z_dev(o) for o in by_distance(NZ)] + [q_dev(o) for o in by_distance(NQ)]
    partners += [core_of(to, 1 - core) for to in z_next + line_next]
    for partner in partners:
        pl.semaphore_signal(barrier, inc=1, device_id=partner, device_id_type=MESH)
    loads = [
        pltpu.make_async_copy(rounding, round_v, in_sem.at[0]),
        pltpu.make_async_copy(codes, codes_v, in_sem.at[1]),
        pltpu.make_async_copy(expo, expo_v, in_sem.at[2]),
    ]
    for load in loads:
        load.start()
    for s in range(NZ):
        at = pl.multiple_of(x * (NZ * blk) + s * blk, 16)
        pltpu.make_async_copy(target.at[pl.ds(at, blk)], tgt.at[s], tgt_sem).start()

    def token_half(h):
        return tokens.at[:, aligned(h, kh)]

    def own_rows(c_):
        return pl.ds(pl.multiple_of(yl * blk + c_ * rows, 16), rows)

    local = pltpu.make_async_copy(token_half(core), xs.at[z, own_rows(core)], loc_sem)
    local.start()

    pl.semaphore_wait(barrier, len(partners))

    mine = xs.at[z, own_rows(core)]
    for k, to in enumerate(z_next):
        for h in range(NC):
            copy(token_half(h), mine, zf.at[k, 0], tz.at[k, core], core_of(to, h)).start()
    for side, to in enumerate(line_next):

        @pl.when(has_next[side])
        def _(side=side, to=to):
            for h in range(NC):
                copy(token_half(h), mine, bs.at[side, yl], tl.at[side, core], core_of(to, h)).start()

    send_t = copy(token_half(1 - core), mine, ts, tr, sib)
    send_t.start()

    def both_cores(s, y_, sems):
        for c_ in range(NC):
            at = pl.ds(pl.multiple_of(y_ * blk + c_ * rows, 16), rows)
            same(xs.at[s, at], ts, sems.at[c_], sib).wait_recv()

    def piece(s, y_):
        return xs.at[s, aligned(y_, blk)]

    def a_piece(s, y_):
        return xs.at[s, aligned(y_, blk), pl.ds(0, a_cols)]

    def b_piece(s, y_):
        return xs.at[s, aligned(y_, blk), pl.ds(a_cols, B_COLS)]

    def place(p):
        found = yl
        for at in range(NYL):
            order = sorted(range(NYL), key=lambda y_: (abs(y_ - at), y_))
            found = jnp.where(yl == at, order[p], found)
        return found

    def z_send(s, j, y_, d, k):
        if j == 0:
            same(piece(s, y_), zf.at[k, d], zr.at[s, y_], z_next[k]).start()
        else:
            same(a_piece(s, y_), za.at[k, d], zr.at[s, y_], z_next[k]).start()

    def z_wait(s, j, y_):
        same((a_piece if j else piece)(s, y_), zf.at[0, 0], zr.at[s, y_], sib).wait_recv()

    def line_send(y_, side):
        @pl.when(has_next[side])
        def _():
            same(piece(z, y_), bs.at[side, y_], br.at[z, y_], line_next[side]).start()

    def line_pass(j, then):
        for side in range(2):
            y_ = yl - j if side == 0 else yl + j

            @pl.when(y_ >= 0 if side == 0 else y_ < NYL)
            def _(side=side, y_=y_):
                if j == 1:
                    both_cores(z, y_, tl.at[side])
                else:
                    same(piece(z, y_), bs.at[side, y_], br.at[z, y_], sib).wait_recv()
                line_send(y_, side)
                then(y_)

    def red_send(i, st, value):
        red_src[i, st] = value
        for o in by_distance((NQ, NY, NZ)[st]):
            to = (q_dev, y_dev, z_dev)[st](o)
            copy(red_src.at[i, st], red_buf.at[i, st, o - 1], rs.at[i, st], rr.at[i, st], to).start()

    def red_got(i, st):
        n = (NQ, NY, NZ)[st] - 1
        return same(red_buf.at[i, st, pl.ds(0, n)], rs.at[i, st], rr.at[i, st], sib)

    def red_recv(i, st):
        red_got(i, st).wait_recv()
        total = red_src[i, st]
        for o in range((NQ, NY, NZ)[st] - 1):
            total += red_buf[i, st, o]
        return total

    def fold(a):
        return a.reshape(a.shape[0] // 8, 8, a.shape[1]).sum(axis=0)

    for load in loads:
        load.wait()
    scale_v[...] = jnp.exp2(expo_v[...].astype(F32)) * D ** (-0.5)

    def group_weights(g, total):
        at = aligned(g, GROUP)
        r = round_v[at]
        sigma = jax.nn.sigmoid(r)
        soft = jnp.clip(sigma * (STRETCH_HIGH - STRETCH_LOW) + STRETCH_LOW, 0.0, 1.0)
        slope = jnp.where(jnp.abs(r) < LIMIT, (STRETCH_HIGH - STRETCH_LOW) * sigma * (1.0 - sigma), 0.0)
        scale = scale_v[pl.ds(g, 1)]
        w_full[at] = (scale * (codes_v[at].astype(F32) + soft)).astype(BF16)
        centered = 2.0 * soft - 1.0
        cube = centered * centered * centered
        ss[at] = scale * slope
        reg[at] = -REG_WEIGHT * 8.0 * cube * slope
        return total + fold(1.0 - cube * centered)

    def half_rows(h):
        return aligned(h, kh)

    def weights(h, total):
        return lax.fori_loop(h * groups, (h + 1) * groups, group_weights, total)

    w_cols = w.at[:, aligned(core, cols)]
    regular = weights(1 - core, jnp.zeros((8, cols), F32))
    send_w = copy(w_full.at[half_rows(1 - core)], w_cols, ws, wr, sib)
    send_w.start()
    send_slopes = [
        copy(ref.at[half_rows(1 - core)], other, fs.at[i], fr.at[i], sib)
        for i, (ref, other) in enumerate(((ss, ss_sib), (reg, reg_sib)))
    ]
    for send in send_slopes:
        send.start()
    regular = weights(core, regular)
    local_w = pltpu.make_async_copy(w_full.at[half_rows(core)], w_cols, wl_sem)
    local_w.start()

    pltpu.make_async_copy(tgt, tgt, tgt_sem).wait()
    err[...] = jnp.zeros_like(err)
    energy = jnp.zeros((8, cols), F32)
    for s in range(NZ):
        t = tgt[s].astype(F32)
        energy += fold(t * t)
    red_send(0, 0, energy)
    gacc[...] = jnp.zeros_like(gacc)

    own_cols, sib_cols = aligned(core, cols), aligned(1 - core, cols)
    own_x = aligned(x, blk)

    def t1(s):
        def rows_of(j, carry):
            at = aligned(j, blk)
            part[s, at] = jnp.dot(xs[s, at], w[...], preferred_element_type=F32)
            return carry

        lax.fori_loop(0, NYL, rows_of, 0, unroll=True)
        copy(part.at[s, :, sib_cols], sbuf.at[s], s1s.at[s], s1r.at[s], sib).start()

    def t2(s):
        same(sbuf.at[s], s1s.at[s], s1r.at[s], sib).wait_recv()
        sbuf[s] = sbuf[s] + part[s, :, own_cols]
        for o in by_distance(NX):
            src = sbuf.at[s, aligned(rem(x + o, NX), blk)]
            copy(src, rbuf.at[s, o - 1], s2s.at[s], s2r.at[s], x_dev(o)).start()

    def t3(s):
        same(rbuf.at[s], s2s.at[s], s2r.at[s], sib).wait_recv()
        total = sbuf[s, own_x]
        for o in range(NX - 1):
            total += rbuf[s, o]
        r2[s] = total
        copy(r2.at[s], r3.at[s], s3s.at[s], s3r.at[s], y_peer).start()

    def t4(s):
        same(r3.at[s], s3s.at[s], s3r.at[s], y_peer).wait_recv()
        pre = r2[s] + r3[s]
        sigma = jax.nn.sigmoid(pre)
        diff = pre * sigma - tgt[s].astype(F32)
        up[s, own_x, own_cols] = (2.0 * diff * sigma * (1.0 + pre * (1.0 - sigma))).astype(BF16)
        for o in by_distance(NQ):
            same(up.at[s, own_x, own_cols], s4s.at[s], s4r.at[s], q_dev(o)).start()
        err[...] += fold(diff * diff)

    def seven(s):
        return same(up.at[s, pl.ds(0, (NQ - 1) * blk // NC)], s4s.at[s], s4r.at[s], sib)

    wide = min(kh, 256)

    def t5(s):
        seven(s).wait_recv()
        u = up[s].T

        def cols_of(i, carry):
            at = aligned(i, wide)
            gacc[:, at] += jnp.dot(u, xs[s, :, at], preferred_element_type=F32)
            return carry

        lax.fori_loop(0, kh // wide, cols_of, 0, unroll=True)

    def each(d, stage):
        def go(i, carry):
            (t1, t2, t3, t4, t5)[stage - 1](rem(z + NZ + (2 * i - 1) * d, NZ))
            return carry

        lax.fori_loop(0, jnp.where(d > 0, 2, jnp.where(d == 0, 1, 0)), go, 0)

    def at_far(back, stage):
        if back:
            each(jnp.int32(last - back), stage)
        else:
            (t1, t2, t3, t4, t5)[stage - 1](far)

    def energy_stage(st):
        if st < 3:
            red_send(0, st, red_recv(0, st - 1))
        else:
            total = red_recv(0, 2)
            energy_v[...] = jnp.broadcast_to(jnp.sum(total, axis=(0, 1), keepdims=True) * (1.0 / NYH), energy_v.shape)

    def tick(d, j, first=False):
        slabs = rem(z + NZ - d, NZ), rem(z + d, NZ)
        y_ = place(j)
        for k in range(2):
            if first:
                both_cores(slabs[k], y_, tz.at[k])
            else:
                z_wait(slabs[k], j, y_)
            if (j < NYL // 2) == (k == 0):
                z_send(slabs[k], j, y_, d, k)
            else:
                pl.when(d < last - 1)(functools.partial(z_send, slabs[k], j, y_, d, k))
        if j == 0:
            for s in slabs:
                for o in range(1, NYL):
                    to = dev(x, yh, rem(yl + o, NYL), z, core)
                    same(b_piece(s, yl), bb.at[s, o], br.at[s, yl], to).start()
        if j == NYL - 1:
            for s in slabs:
                for o in range(1, NYL):
                    at = rem(yl + o, NYL)
                    same(b_piece(s, at), bb.at[s, o], br.at[s, at], sib).wait_recv()

            @pl.when(d == last - 1)
            def _():
                for i in range(1, NYL):
                    k = 0 if i < NYL // 2 else 1
                    at = place(i)
                    same(b_piece(slabs[k], at), zb.at[k], br.at[slabs[k], at], z_next[k]).start()

    for j in range(1, NYL):

        def onward(y_):
            for k in range(2):
                z_send(z, 1, y_, 0, k)

        line_pass(j, onward)
        tick(jnp.int32(1), j - 1, j == 1)
    local_w.wait()
    send_w.wait_recv()
    local.wait()
    copy(token_half(1 - core), xs.at[z, own_rows(1 - core)], ts, tr, sib).wait_recv()
    t1(z)
    tick(jnp.int32(1), NYL - 1)
    energy_stage(1)
    t2(z)
    for back, stage in PLAN[NYL - 1]:
        if back == 0:
            each(jnp.int32(1), stage)

    def step(d, carry):
        for j in range(NYL):
            tick(d, j)
            if j == 0:
                pl.when(d == 2)(functools.partial(t3, z))
            for back, stage in PLAN[j]:
                each(d - back, stage)
            if j == NYL - 1:
                for st in range(2, 4):
                    if st < last:
                        pl.when(d == st)(functools.partial(energy_stage, st))
        return carry

    lax.fori_loop(2, last, step, 0)

    far = rem(z + last, NZ)
    for work in BEFORE_FAR:
        at_far(*work)
    for j in range(NYL // 2):
        for jj in (j, j + NYL // 2):
            z_wait(far, jj, place(jj))
        for work in FAR[j]:
            at_far(*work)
    for j in range(1, NYL):
        at = rem(yl + j, NYL)
        same(b_piece(far, at), zb.at[0], br.at[far, at], sib).wait_recv()
    if last == 2:
        t3(z)
    for st in range(last, 4):
        energy_stage(st)
    for work in TAIL:
        at_far(*work)

    factor = float(D * FW) / energy_v[0:1, 0:1]
    for send in send_slopes:
        send.wait_recv()

    def finish(first, slopes, reg_ref, into, base):
        def go(i, total):
            at = aligned(base + i, GROUP)
            g = factor * (slopes[at] * gacc[pl.ds(first, cols), aligned(i, GROUP)].T) + reg_ref[at]
            into[at] = g
            return total + fold(g * g)

        return functools.partial(lax.fori_loop, 0, groups, go, unroll=True)

    sib_first, own_first = (pl.multiple_of(c_ * cols, cols) for c_ in (1 - core, core))
    squares = finish(sib_first, ss_sib, reg_sib, grad_sib, 0)(jnp.zeros((8, cols), F32))
    send_g = copy(grad_sib, grad.at[half_rows(core)], gs, gr, sib)
    send_g.start()
    squares = finish(own_first, ss, reg, grad, core * groups)(squares)

    row = lax.broadcasted_iota(jnp.int32, (8, cols), 0)
    parts = [jnp.sum(v, axis=0, keepdims=True) for v in (squares, err[...] * (1.0 / NYH), regular)]
    tile = jnp.zeros((8, cols), F32)
    for i, v in enumerate(parts):
        tile = jnp.where(row == i, v, tile)
    red_send(1, 0, tile)
    send_g.wait_recv()
    red_send(1, 1, red_recv(1, 0))
    red_send(1, 2, red_recv(1, 1))
    sums = jnp.sum(red_recv(1, 2), axis=1, keepdims=True)
    rms = jnp.sqrt(sums[0:1] / float(D * FW) + EPSILON)
    inverse[...] = STEP_SIZE / rms
    loss[...] = sums[1:2] / energy_v[0:1, 0:1] + REG_WEIGHT * sums[2:3] / float(D * FW)

    send_t.wait_send()
    for k in range(2):
        for d in range(last):
            n = NYL - 1
            if d < last - 1 or k == 0:
                same(piece(z, yl), zf.at[k, d], zr.at[z, yl], sib).wait_send()
            if d == last - 1:
                n = NYL // 2 - 1 if k == 0 else NYL - NYL // 2
                if n:
                    same(xs.at[z, pl.ds(0, n * blk), pl.ds(0, B_COLS)], zb.at[k], zr.at[z, yl], sib).wait_send()
            if n:
                same(xs.at[z, pl.ds(0, n * blk), pl.ds(0, a_cols)], za.at[k, d], zr.at[z, yl], sib).wait_send()

    for side in range(2):
        for y_ in range(NYL):

            @pl.when(jnp.logical_and(has_next[side], y_ <= yl if side == 0 else y_ >= yl))
            def _(side=side, y_=y_):
                same(piece(z, y_), bs.at[side, y_], br.at[z, y_], sib).wait_send()

    def sent_far_line(d, carry):
        for s in (rem(z + NZ - d, NZ), rem(z + d, NZ)):
            for o in range(1, NYL):
                same(b_piece(s, yl), bb.at[s, o], br.at[s, yl], sib).wait_send()
        return carry

    lax.fori_loop(1, last, sent_far_line, 0)
    send_w.wait_send()
    send_g.wait_send()
    for send in send_slopes:
        send.wait_send()

    def sent_stages(s, carry):
        same(sbuf.at[s], s1s.at[s], s1r.at[s], sib).wait_send()
        same(rbuf.at[s], s2s.at[s], s2r.at[s], sib).wait_send()
        same(r3.at[s], s3s.at[s], s3r.at[s], y_peer).wait_send()
        seven(s).wait_send()
        return carry

    lax.fori_loop(0, NZ, sent_stages, 0)
    for i in range(2):
        for st in range(3):
            red_got(i, st).wait_send()


def local(tokens, codes, expo, rounding, target):
    rows, kd = tokens.shape
    cols = codes.shape[1]
    kh = kd // NC
    blk = rows * NC
    slab = NYL * blk
    dma = pltpu.SemaphoreType.DMA
    vmem = pltpu.VMEM
    grad, inverse, loss = pl.pallas_call(
        kernel,
        out_shape=(
            jax.ShapeDtypeStruct(rounding.shape, F32),
            jax.ShapeDtypeStruct((1, 1), F32),
            jax.ShapeDtypeStruct((1, 1), F32),
        ),
        in_specs=[pl.BlockSpec(memory_space=pl.ANY)] * 5,
        out_specs=(pl.BlockSpec(memory_space=pltpu.VMEM),) * 3,
        scratch_shapes=[
            vmem((NZ, slab, kh), BF16),
            vmem((kd, cols), jnp.int32),
            vmem(expo.shape, jnp.int32),
            vmem((kd, cols), F32),
            vmem((NZ, blk, cols), BF16),
            vmem(expo.shape, F32),
            vmem((kd, cols), F32),
            vmem((kd, cols), F32),
            vmem((kh, cols), F32),
            vmem((kh, cols), F32),
            vmem((kh, cols), F32),
            vmem((kd, cols), BF16),
            vmem((kh, NC * cols), BF16),
            vmem((NZ, slab, NC * cols), F32),
            vmem((NZ, slab, cols), F32),
            vmem((NZ, NX - 1, blk, cols), F32),
            vmem((NZ, blk, cols), F32),
            vmem((NZ, blk, cols), F32),
            vmem((NZ, slab, NC * cols), BF16),
            vmem((NC * cols, kh), F32),
            vmem((8, cols), F32),
            vmem((2, 3, 8, cols), F32),
            vmem((2, 3, max(NQ, NY, NZ) - 1, 8, cols), F32),
            vmem((8, cols), F32),
            dma((3,)), dma, dma, dma,
            dma, dma, dma((2, NC)), dma((2, NC)), dma((2, NYL)), dma((NZ, NYL)), dma((NZ, NYL)), dma((2, NZ // 2)), dma((2, NZ // 2)), dma((2,)), dma((NZ, NYL)), dma, dma,
            dma((2,)), dma((2,)), dma((NZ,)), dma((NZ,)), dma((NZ,)), dma((NZ,)), dma((NZ,)), dma((NZ,)), dma((NZ,)), dma((NZ,)),
            dma, dma, dma((2, 3)), dma((2, 3)),
        ],
        compiler_params=pltpu.CompilerParams(
            collective_id=0, has_side_effects=True, vmem_limit_bytes=VMEM_LIMIT
        ),
    )(tokens, codes, expo, rounding, target)
    return rounding - grad * inverse, loss.reshape(())


def solution(mesh):
    in_specs = (P("dp", "mp"), P("mp", "dp"), P("mp", "dp"), P("mp", "dp"), P(None, "dp"))
    out_specs = (P("mp", "dp"), P())
    return jax.shard_map(local, mesh=mesh, in_specs=in_specs, out_specs=out_specs, check_vma=False)
```

```python
import functools

import jax
import jax.numpy as jnp
from jax import lax
from jax.experimental import pallas as pl
from jax.experimental.pallas import tpu as pltpu
from jax.sharding import PartitionSpec as P

D = 16384
FW = 8192
GROUP = 128
STRETCH_HIGH = 1.1
STRETCH_LOW = -0.1
LIMIT = 2.3978952727983707
REG_WEIGHT = 0.01
STEP_SIZE = 0.5
EPSILON = 1e-06

NX, NYL, NYH, NZ, NC = 4, 4, 2, 8, 2
NQ = NX * NC
NY = NYL * NYH
B_COLS = 128

PLAN = (((1, 2),), ((3, 5),), ((1, 3),), ((2, 4), (0, 1)))
BEFORE_FAR = ((1, 2),)
FAR = (((2, 4), (3, 5)), ())
TAIL = ((0, 1), (1, 3), (0, 2), (2, 5), (0, 3), (1, 4), (0, 4), (1, 5), (0, 5))
MESH = pl.DeviceIdType.MESH


def by_distance(n):
    return sorted(range(1, n), key=lambda o: -min(o, n - o))


VMEM_LIMIT = 60 << 20
F32 = jnp.float32
BF16 = jnp.bfloat16


def rem(a, n):
    return lax.rem(a, jnp.int32(n))


def div(a, n):
    return lax.div(a, jnp.int32(n))


def aligned(a, n):
    return pl.ds(pl.multiple_of(a * n, n), n)


def kernel(
    tokens, codes, expo, rounding, target, grad, inverse, loss,
    xs, codes_v, expo_v, round_v, tgt, scale_v, ss, reg, ss_sib, reg_sib, grad_sib, w_full, w, part, sbuf, rbuf, r2, r3, up, gacc,
    err, red_src, red_buf, energy_v,
    in_sem, tgt_sem, loc_sem, wl_sem,
    ts, tr, tz, tl, bs, bb, br, zf, za, zb, zr, ws, wr, fs, fr, s1s, s1r, s2s, s2r, s3s, s3r, s4s, s4r, gs, gr, rs, rr,
):
    dp, mp = lax.axis_index("dp"), lax.axis_index("mp")
    core = rem(dp, NC)
    z = rem(div(dp, NC), NZ)
    yl = div(dp, NC * NZ)
    x = rem(mp, NX)
    yh = div(mp, NX)
    q = x * NC + core
    y = yh * NYL + yl

    def dev(x_, yh_, yl_, z_, c_):
        return ((yl_ * NZ + z_) * NC + c_, yh_ * NX + x_)

    rows, kd = tokens.shape
    kh = kd // NC
    blk = rows * NC
    cols = codes.shape[1]
    groups = kh // GROUP
    a_cols = kh - B_COLS
    last = NZ // 2

    def q_dev(o):
        t = rem(q + o, NQ)
        return dev(div(t, NC), yh, yl, z, rem(t, NC))

    def y_dev(o):
        t = rem(y + o, NY)
        return dev(x, div(t, NYL), rem(t, NYL), z, core)

    def z_dev(o):
        return dev(x, yh, yl, rem(z + o, NZ), core)

    def x_dev(o):
        return dev(rem(x + o, NX), yh, yl, z, core)

    z_next = (z_dev(1), z_dev(NZ - 1))
    line_next = (dev(x, yh, rem(yl + 1, NYL), z, core), dev(x, yh, rem(yl + NYL - 1, NYL), z, core))
    has_next = (yl < NYL - 1, yl > 0)
    sib = dev(x, yh, yl, z, 1 - core)
    y_peer = dev(x, 1 - yh, yl, z, core)

    def copy(src, dst, ssem, rsem, to):
        return pltpu.make_async_remote_copy(
            src_ref=src, dst_ref=dst, send_sem=ssem, recv_sem=rsem, device_id=to, device_id_type=MESH
        )

    def core_of(to, c_):
        return (to[0] - core + c_, to[1])

    def same(ref, ssem, rsem, to):
        return copy(ref, ref, ssem, rsem, to)

    barrier = pltpu.get_barrier_semaphore()
    partners = [y_dev(o) for o in by_distance(NY)] + [z_dev(o) for o in by_distance(NZ)] + [q_dev(o) for o in by_distance(NQ)]
    partners += [core_of(to, 1 - core) for to in z_next + line_next]
    for partner in partners:
        pl.semaphore_signal(barrier, inc=1, device_id=partner, device_id_type=MESH)
    loads = [
        pltpu.make_async_copy(rounding, round_v, in_sem.at[0]),
        pltpu.make_async_copy(codes, codes_v, in_sem.at[1]),
        pltpu.make_async_copy(expo, expo_v, in_sem.at[2]),
    ]
    for load in loads:
        load.start()
    for s in range(NZ):
        at = pl.multiple_of(x * (NZ * blk) + s * blk, 16)
        pltpu.make_async_copy(target.at[pl.ds(at, blk)], tgt.at[s], tgt_sem).start()

    def token_half(h):
        return tokens.at[:, aligned(h, kh)]

    def own_rows(c_):
        return pl.ds(pl.multiple_of(yl * blk + c_ * rows, 16), rows)

    local = pltpu.make_async_copy(token_half(core), xs.at[z, own_rows(core)], loc_sem)
    local.start()

    pl.semaphore_wait(barrier, len(partners))

    mine = xs.at[z, own_rows(core)]
    for k, to in enumerate(z_next):
        for h in range(NC):
            copy(token_half(h), mine, zf.at[k, 0], tz.at[k, core], core_of(to, h)).start()
    for side, to in enumerate(line_next):

        @pl.when(has_next[side])
        def _(side=side, to=to):
            for h in range(NC):
                copy(token_half(h), mine, bs.at[side, yl], tl.at[side, core], core_of(to, h)).start()

    send_t = copy(token_half(1 - core), mine, ts, tr, sib)
    send_t.start()

    def both_cores(s, y_, sems):
        for c_ in range(NC):
            at = pl.ds(pl.multiple_of(y_ * blk + c_ * rows, 16), rows)
            same(xs.at[s, at], ts, sems.at[c_], sib).wait_recv()

    def piece(s, y_):
        return xs.at[s, aligned(y_, blk)]

    def a_piece(s, y_):
        return xs.at[s, aligned(y_, blk), pl.ds(0, a_cols)]

    def b_piece(s, y_):
        return xs.at[s, aligned(y_, blk), pl.ds(a_cols, B_COLS)]

    def place(p):
        found = yl
        for at in range(NYL):
            order = sorted(range(NYL), key=lambda y_: (abs(y_ - at), y_))
            found = jnp.where(yl == at, order[p], found)
        return found

    def z_send(s, j, y_, d, k):
        if j == 0:
            same(piece(s, y_), zf.at[k, d], zr.at[s, y_], z_next[k]).start()
        else:
            same(a_piece(s, y_), za.at[k, d], zr.at[s, y_], z_next[k]).start()

    def z_wait(s, j, y_):
        same((a_piece if j else piece)(s, y_), zf.at[0, 0], zr.at[s, y_], sib).wait_recv()

    def line_send(y_, side):
        @pl.when(has_next[side])
        def _():
            same(piece(z, y_), bs.at[side, y_], br.at[z, y_], line_next[side]).start()

    def line_pass(j, then):
        for side in range(2):
            y_ = yl - j if side == 0 else yl + j

            @pl.when(y_ >= 0 if side == 0 else y_ < NYL)
            def _(side=side, y_=y_):
                if j == 1:
                    both_cores(z, y_, tl.at[side])
                else:
                    same(piece(z, y_), bs.at[side, y_], br.at[z, y_], sib).wait_recv()
                line_send(y_, side)
                then(y_)

    def red_send(i, st, value):
        red_src[i, st] = value
        for o in by_distance((NQ, NY, NZ)[st]):
            to = (q_dev, y_dev, z_dev)[st](o)
            copy(red_src.at[i, st], red_buf.at[i, st, o - 1], rs.at[i, st], rr.at[i, st], to).start()

    def red_got(i, st):
        n = (NQ, NY, NZ)[st] - 1
        return same(red_buf.at[i, st, pl.ds(0, n)], rs.at[i, st], rr.at[i, st], sib)

    def red_recv(i, st):
        red_got(i, st).wait_recv()
        total = red_src[i, st]
        for o in range((NQ, NY, NZ)[st] - 1):
            total += red_buf[i, st, o]
        return total

    def fold(a):
        return a.reshape(a.shape[0] // 8, 8, a.shape[1]).sum(axis=0)

    for load in loads:
        load.wait()
    scale_v[...] = jnp.exp2(expo_v[...].astype(F32)) * D ** (-0.5)

    def group_weights(g, total):
        at = aligned(g, GROUP)
        r = round_v[at]
        sigma = jax.nn.sigmoid(r)
        soft = jnp.clip(sigma * (STRETCH_HIGH - STRETCH_LOW) + STRETCH_LOW, 0.0, 1.0)
        slope = jnp.where(jnp.abs(r) < LIMIT, (STRETCH_HIGH - STRETCH_LOW) * sigma * (1.0 - sigma), 0.0)
        scale = scale_v[pl.ds(g, 1)]
        w_full[at] = (scale * (codes_v[at].astype(F32) + soft)).astype(BF16)
        centered = 2.0 * soft - 1.0
        cube = centered * centered * centered
        ss[at] = scale * slope
        reg[at] = -REG_WEIGHT * 8.0 * cube * slope
        return total + fold(1.0 - cube * centered)

    def half_rows(h):
        return aligned(h, kh)

    def weights(h, total):
        return lax.fori_loop(0, groups, lambda i, t: group_weights(h * groups + i, t), total, unroll=2)

    w_cols = w.at[:, aligned(core, cols)]
    regular = weights(1 - core, jnp.zeros((8, cols), F32))
    send_w = copy(w_full.at[half_rows(1 - core)], w_cols, ws, wr, sib)
    send_w.start()
    send_slopes = [
        copy(ref.at[half_rows(1 - core)], other, fs.at[i], fr.at[i], sib)
        for i, (ref, other) in enumerate(((ss, ss_sib), (reg, reg_sib)))
    ]
    for send in send_slopes:
        send.start()
    regular = weights(core, regular)
    local_w = pltpu.make_async_copy(w_full.at[half_rows(core)], w_cols, wl_sem)
    local_w.start()

    pltpu.make_async_copy(tgt, tgt, tgt_sem).wait()
    err[...] = jnp.zeros_like(err)
    energy = jnp.zeros((8, cols), F32)
    for s in range(NZ):
        t = tgt[s].astype(F32)
        energy += fold(t * t)
    red_send(0, 0, energy)
    gacc[...] = jnp.zeros_like(gacc)

    own_cols, sib_cols = aligned(core, cols), aligned(1 - core, cols)
    own_x = aligned(x, blk)

    def t1(s):
        def rows_of(j, carry):
            at = aligned(j, blk)
            part[s, at] = jnp.dot(xs[s, at], w[...], preferred_element_type=F32)
            return carry

        lax.fori_loop(0, NYL, rows_of, 0, unroll=True)
        copy(part.at[s, :, sib_cols], sbuf.at[s], s1s.at[s], s1r.at[s], sib).start()

    def t2(s):
        same(sbuf.at[s], s1s.at[s], s1r.at[s], sib).wait_recv()
        sbuf[s] = sbuf[s] + part[s, :, own_cols]
        for o in by_distance(NX):
            src = sbuf.at[s, aligned(rem(x + o, NX), blk)]
            copy(src, rbuf.at[s, o - 1], s2s.at[s], s2r.at[s], x_dev(o)).start()

    def t3(s):
        same(rbuf.at[s], s2s.at[s], s2r.at[s], sib).wait_recv()
        total = sbuf[s, own_x]
        for o in range(NX - 1):
            total += rbuf[s, o]
        r2[s] = total
        copy(r2.at[s], r3.at[s], s3s.at[s], s3r.at[s], y_peer).start()

    def t4(s):
        same(r3.at[s], s3s.at[s], s3r.at[s], y_peer).wait_recv()
        pre = r2[s] + r3[s]
        sigma = jax.nn.sigmoid(pre)
        diff = pre * sigma - tgt[s].astype(F32)
        up[s, own_x, own_cols] = (2.0 * diff * sigma * (1.0 + pre * (1.0 - sigma))).astype(BF16)
        for o in by_distance(NQ):
            same(up.at[s, own_x, own_cols], s4s.at[s], s4r.at[s], q_dev(o)).start()
        err[...] += fold(diff * diff)

    def seven(s):
        return same(up.at[s, pl.ds(0, (NQ - 1) * blk // NC)], s4s.at[s], s4r.at[s], sib)

    wide = min(kh, 256)

    def t5(s):
        seven(s).wait_recv()
        u = up[s].T

        def cols_of(i, carry):
            at = aligned(i, wide)
            gacc[:, at] += jnp.dot(u, xs[s, :, at], preferred_element_type=F32)
            return carry

        lax.fori_loop(0, kh // wide, cols_of, 0, unroll=True)

    def each(d, stage):
        def go(i, carry):
            (t1, t2, t3, t4, t5)[stage - 1](rem(z + NZ + (2 * i - 1) * d, NZ))
            return carry

        lax.fori_loop(0, jnp.where(d > 0, 2, jnp.where(d == 0, 1, 0)), go, 0)

    def at_far(back, stage):
        if back:
            each(jnp.int32(last - back), stage)
        else:
            (t1, t2, t3, t4, t5)[stage - 1](far)

    def energy_stage(st):
        if st < 3:
            red_send(0, st, red_recv(0, st - 1))
        else:
            total = red_recv(0, 2)
            energy_v[...] = jnp.broadcast_to(jnp.sum(total, axis=(0, 1), keepdims=True) * (1.0 / NYH), energy_v.shape)

    def tick(d, j, first=False):
        slabs = rem(z + NZ - d, NZ), rem(z + d, NZ)
        y_ = place(j)
        for k in range(2):
            if first:
                both_cores(slabs[k], y_, tz.at[k])
            else:
                z_wait(slabs[k], j, y_)
            if (j < NYL // 2) == (k == 0):
                z_send(slabs[k], j, y_, d, k)
            else:
                pl.when(d < last - 1)(functools.partial(z_send, slabs[k], j, y_, d, k))
        if j == 0:
            for s in slabs:
                for o in range(1, NYL):
                    to = dev(x, yh, rem(yl + o, NYL), z, core)
                    same(b_piece(s, yl), bb.at[s, o], br.at[s, yl], to).start()
        if j == NYL - 1:
            for s in slabs:
                for o in range(1, NYL):
                    at = rem(yl + o, NYL)
                    same(b_piece(s, at), bb.at[s, o], br.at[s, at], sib).wait_recv()

            @pl.when(d == last - 1)
            def _():
                for i in range(1, NYL):
                    k = 0 if i < NYL // 2 else 1
                    at = place(i)
                    same(b_piece(slabs[k], at), zb.at[k], br.at[slabs[k], at], z_next[k]).start()

    for j in range(1, NYL):

        def onward(y_):
            for k in range(2):
                z_send(z, 1, y_, 0, k)

        line_pass(j, onward)
        tick(jnp.int32(1), j - 1, j == 1)
    local_w.wait()
    send_w.wait_recv()
    local.wait()
    copy(token_half(1 - core), xs.at[z, own_rows(1 - core)], ts, tr, sib).wait_recv()
    t1(z)
    tick(jnp.int32(1), NYL - 1)
    energy_stage(1)
    t2(z)
    for back, stage in PLAN[NYL - 1]:
        if back == 0:
            each(jnp.int32(1), stage)

    def step(d, carry):
        for j in range(NYL):
            tick(d, j)
            if j == 0:
                pl.when(d == 2)(functools.partial(t3, z))
            for back, stage in PLAN[j]:
                each(d - back, stage)
            if j == NYL - 1:
                for st in range(2, 4):
                    if st < last:
                        pl.when(d == st)(functools.partial(energy_stage, st))
        return carry

    lax.fori_loop(2, last, step, 0)

    far = rem(z + last, NZ)
    for work in BEFORE_FAR:
        at_far(*work)
    for j in range(NYL // 2):
        for jj in (j, j + NYL // 2):
            z_wait(far, jj, place(jj))
        for work in FAR[j]:
            at_far(*work)
    for j in range(1, NYL):
        at = rem(yl + j, NYL)
        same(b_piece(far, at), zb.at[0], br.at[far, at], sib).wait_recv()
    if last == 2:
        t3(z)
    for st in range(last, 4):
        energy_stage(st)
    for work in TAIL:
        at_far(*work)

    factor = float(D * FW) / energy_v[0:1, 0:1]
    for send in send_slopes:
        send.wait_recv()

    def finish(first, slopes, reg_ref, into, base):
        def go(i, total):
            at = aligned(base + i, GROUP)
            g = factor * (slopes[at] * gacc[pl.ds(first, cols), aligned(i, GROUP)].T) + reg_ref[at]
            into[at] = g
            return total + fold(g * g)

        return functools.partial(lax.fori_loop, 0, groups, go, unroll=True)

    sib_first, own_first = (pl.multiple_of(c_ * cols, cols) for c_ in (1 - core, core))
    squares = finish(sib_first, ss_sib, reg_sib, grad_sib, 0)(jnp.zeros((8, cols), F32))
    send_g = copy(grad_sib, grad.at[half_rows(core)], gs, gr, sib)
    send_g.start()
    squares = finish(own_first, ss, reg, grad, core * groups)(squares)

    row = lax.broadcasted_iota(jnp.int32, (8, cols), 0)
    parts = [jnp.sum(v, axis=0, keepdims=True) for v in (squares, err[...] * (1.0 / NYH), regular)]
    tile = jnp.zeros((8, cols), F32)
    for i, v in enumerate(parts):
        tile = jnp.where(row == i, v, tile)
    red_send(1, 0, tile)
    send_g.wait_recv()
    red_send(1, 1, red_recv(1, 0))
    red_send(1, 2, red_recv(1, 1))
    sums = jnp.sum(red_recv(1, 2), axis=1, keepdims=True)
    rms = jnp.sqrt(sums[0:1] / float(D * FW) + EPSILON)
    inverse[...] = STEP_SIZE / rms
    loss[...] = sums[1:2] / energy_v[0:1, 0:1] + REG_WEIGHT * sums[2:3] / float(D * FW)

    send_t.wait_send()
    for k in range(2):
        for d in range(last):
            n = NYL - 1
            if d < last - 1 or k == 0:
                same(piece(z, yl), zf.at[k, d], zr.at[z, yl], sib).wait_send()
            if d == last - 1:
                n = NYL // 2 - 1 if k == 0 else NYL - NYL // 2
                if n:
                    same(xs.at[z, pl.ds(0, n * blk), pl.ds(0, B_COLS)], zb.at[k], zr.at[z, yl], sib).wait_send()
            if n:
                same(xs.at[z, pl.ds(0, n * blk), pl.ds(0, a_cols)], za.at[k, d], zr.at[z, yl], sib).wait_send()

    for side in range(2):
        for y_ in range(NYL):

            @pl.when(jnp.logical_and(has_next[side], y_ <= yl if side == 0 else y_ >= yl))
            def _(side=side, y_=y_):
                same(piece(z, y_), bs.at[side, y_], br.at[z, y_], sib).wait_send()

    def sent_far_line(d, carry):
        for s in (rem(z + NZ - d, NZ), rem(z + d, NZ)):
            for o in range(1, NYL):
                same(b_piece(s, yl), bb.at[s, o], br.at[s, yl], sib).wait_send()
        return carry

    lax.fori_loop(1, last, sent_far_line, 0)
    send_w.wait_send()
    send_g.wait_send()
    for send in send_slopes:
        send.wait_send()

    def sent_stages(s, carry):
        same(sbuf.at[s], s1s.at[s], s1r.at[s], sib).wait_send()
        same(rbuf.at[s], s2s.at[s], s2r.at[s], sib).wait_send()
        same(r3.at[s], s3s.at[s], s3r.at[s], y_peer).wait_send()
        seven(s).wait_send()
        return carry

    lax.fori_loop(0, NZ, sent_stages, 0)
    for i in range(2):
        for st in range(3):
            red_got(i, st).wait_send()


def local(tokens, codes, expo, rounding, target):
    rows, kd = tokens.shape
    cols = codes.shape[1]
    kh = kd // NC
    blk = rows * NC
    slab = NYL * blk
    dma = pltpu.SemaphoreType.DMA
    vmem = pltpu.VMEM
    grad, inverse, loss = pl.pallas_call(
        kernel,
        out_shape=(
            jax.ShapeDtypeStruct(rounding.shape, F32),
            jax.ShapeDtypeStruct((1, 1), F32),
            jax.ShapeDtypeStruct((1, 1), F32),
        ),
        in_specs=[pl.BlockSpec(memory_space=pl.ANY)] * 5,
        out_specs=(pl.BlockSpec(memory_space=pltpu.VMEM),) * 3,
        scratch_shapes=[
            vmem((NZ, slab, kh), BF16),
            vmem((kd, cols), jnp.int32),
            vmem(expo.shape, jnp.int32),
            vmem((kd, cols), F32),
            vmem((NZ, blk, cols), BF16),
            vmem(expo.shape, F32),
            vmem((kd, cols), F32),
            vmem((kd, cols), F32),
            vmem((kh, cols), F32),
            vmem((kh, cols), F32),
            vmem((kh, cols), F32),
            vmem((kd, cols), BF16),
            vmem((kh, NC * cols), BF16),
            vmem((NZ, slab, NC * cols), F32),
            vmem((NZ, slab, cols), F32),
            vmem((NZ, NX - 1, blk, cols), F32),
            vmem((NZ, blk, cols), F32),
            vmem((NZ, blk, cols), F32),
            vmem((NZ, slab, NC * cols), BF16),
            vmem((NC * cols, kh), F32),
            vmem((8, cols), F32),
            vmem((2, 3, 8, cols), F32),
            vmem((2, 3, max(NQ, NY, NZ) - 1, 8, cols), F32),
            vmem((8, cols), F32),
            dma((3,)), dma, dma, dma,
            dma, dma, dma((2, NC)), dma((2, NC)), dma((2, NYL)), dma((NZ, NYL)), dma((NZ, NYL)), dma((2, NZ // 2)), dma((2, NZ // 2)), dma((2,)), dma((NZ, NYL)), dma, dma,
            dma((2,)), dma((2,)), dma((NZ,)), dma((NZ,)), dma((NZ,)), dma((NZ,)), dma((NZ,)), dma((NZ,)), dma((NZ,)), dma((NZ,)),
            dma, dma, dma((2, 3)), dma((2, 3)),
        ],
        compiler_params=pltpu.CompilerParams(
            collective_id=0, has_side_effects=True, vmem_limit_bytes=VMEM_LIMIT
        ),
    )(tokens, codes, expo, rounding, target)
    return rounding - grad * inverse, loss.reshape(())


def solution(mesh):
    in_specs = (P("dp", "mp"), P("mp", "dp"), P("mp", "dp"), P("mp", "dp"), P(None, "dp"))
    out_specs = (P("mp", "dp"), P())
    return jax.shard_map(local, mesh=mesh, in_specs=in_specs, out_specs=out_specs, check_vma=False)
```
